512 devices in a mesh: seq: 128 (over y_hi, x, z, core), head: 4 (over y_lo).
Axes of the slice: x: 4, y: 8 (y_hi: 2, y_lo: 4; y = y_hi * 4 + y_lo), z: 8, core: 2. Of those that a mesh axis runs over, the one named last changes fastest.
Arguments:
- shared_qk: bfloat16 [65536, 512], P('seq', 'head'), may hold values from -300 to 300
- value_rows: bfloat16 [65536, 512], P('seq', 'head'), may hold values from -12 to 12
- out_grad: bfloat16 [65536, 512], P('seq', 'head'), may hold values from -6 to 6
- bucket_order: int32 [4, 65536], P('head', 'seq'), may hold values from 0 to 65535, as said below
- inverse_order: int32 [4, 65536], P('head', 'seq'), may hold values from 0 to 65535, as said below
Outputs:
- attended: bfloat16 [65536, 512], P('seq', 'head')
- grad_qk: bfloat16 [65536, 512], P('seq', 'head')
- grad_v: bfloat16 [65536, 512], P('seq', 'head')
The draws below stay inside these ranges and needn't reach their ends.
Inputs may be any that keep to these rules, and one draw needn't show every extreme that they name: `bucket_order`: each row is a permutation of the positions. Cut positions and slots into aligned blocks of 512: for every group and every pair of a position block and a slot block, at most 6 positions of the one have slots in the other, and 6 is reached in every group by some pair for every slot block and every position block. inverse_order[g, bucket_order[g, s]] = s.
All inputs are finite; a program needn't handle non-finite values.
Results may differ from the reference program's by a relative error of at most 0.025.
Values may be sent and summed in bfloat16 or wider, within the bound.
No kernel may reach another device: no remote copies, remote signals or barrier semaphores. Data moves between devices by JAX's collectives and lax.ppermute only.
A program may use at most 64 MiB of HBM per device.

```python
import jax
import jax.numpy as jnp
from jax import lax

HEADS = 8
HEAD_DIM = 64
BLOCK = 512
TOK_DEV = 512
TOKENS = 65536
GROUPS = 4


def bucket_layout(key):
    block_count = TOKENS // TOK_DEV
    base_count = TOK_DEV // block_count
    extra_count = TOK_DEV // (2 * block_count)

    def one_group(group_key):
        key_first, key_shift, key_local, key_shuffle = jax.random.split(group_key, 4)
        first_perm = jax.random.permutation(key_first, block_count)
        offset = jax.random.randint(key_shift, (), 1, block_count)
        second_perm = first_perm[(jnp.arange(block_count) + offset) % block_count]
        columns = jnp.arange(block_count)
        counts = base_count + extra_count * ((columns[None, :] == first_perm[:, None]).astype(jnp.int32) - (columns[None, :] == second_perm[:, None]).astype(jnp.int32))
        cum_incl = jnp.cumsum(counts, axis=1)
        ranks = jnp.arange(TOK_DEV, dtype=jnp.int32)
        target = jnp.sum((cum_incl[:, None, :] <= ranks[None, :, None]).astype(jnp.int32), axis=2)
        cum_excl = cum_incl - counts
        within = ranks[None, :] - jnp.take_along_axis(cum_excl, target, axis=1)
        dest_offset = jnp.cumsum(counts, axis=0) - counts
        pre_slot = jnp.take_along_axis(dest_offset, target, axis=1) + within
        local_order = jax.vmap(lambda sub_key: jax.random.permutation(sub_key, TOK_DEV))(jax.random.split(key_local, block_count))
        shuffle = jax.vmap(lambda sub_key: jax.random.permutation(sub_key, TOK_DEV))(jax.random.split(key_shuffle, block_count))
        final_slot = shuffle[target, pre_slot]
        slot_global = (target * TOK_DEV + final_slot).astype(jnp.int32)
        position = (jnp.arange(block_count)[:, None] * TOK_DEV + local_order).astype(jnp.int32)
        inverse = jnp.zeros((TOKENS,), jnp.int32).at[position.reshape(-1)].set(slot_global.reshape(-1))
        order = jnp.zeros((TOKENS,), jnp.int32).at[inverse].set(jnp.arange(TOKENS, dtype=jnp.int32))
        return (order, inverse)
    return jax.vmap(one_group)(jax.random.split(key, GROUPS))


def draw_bucket_order(key, part):
    order, inverse = bucket_layout(key)
    return order


def draw_inverse_order(key, part):
    order, inverse = bucket_layout(key)
    return inverse


def draw_shared_qk(key, part):
    key = jax.random.fold_in(key, 11)
    key_base = jax.random.fold_in(key, 1)
    shape = (TOKENS, HEADS * HEAD_DIM)
    return (2.0 * jnp.clip(jax.random.normal(key_base, shape, jnp.float32), -6.0, 6.0)).astype(jnp.bfloat16)


def level_of(own_key, extent, cuts, low, largest):
    level, own = 1.0, jax.random.fold_in(own_key, 6)
    for dim, parts in cuts:
        steps = jnp.exp(jax.random.uniform(jax.random.fold_in(own, dim), (parts,), jnp.float32, low / len(cuts), largest / len(cuts)))
        level = level * jnp.repeat(steps, extent[dim] // parts).reshape([-1 if axis == dim else 1 for axis in range(len(extent))])
    return level


def normal_values(own_key, dims, scale, reach, shards=(), held_as=jnp.bfloat16):
    entries = jax.random.normal(own_key, dims, jnp.float32) * scale
    if len(shards) > 0:
        entries = level_of(own_key, dims, shards, -0.22, 0.18) * entries
    return jnp.clip(entries, min=-reach, max=reach).astype(held_as)


def setup_inputs(seed: int = 0) -> dict:
    streams_of = jax.random.split(jax.random.key(seed), 6)
    return {
        "shared_qk": draw_shared_qk(jax.random.fold_in(streams_of[5], 71), 0),
        "value_rows": normal_values(streams_of[1], (TOKENS, HEADS * HEAD_DIM), 2.0, 12.0, ((0, 128), (1, 4))),
        "out_grad": normal_values(streams_of[2], (TOKENS, HEADS * HEAD_DIM), 1.0, 6.0, ((0, 128), (1, 4))),
        "bucket_order": draw_bucket_order(jax.random.fold_in(streams_of[5], 71), 0),
        "inverse_order": draw_inverse_order(jax.random.fold_in(streams_of[5], 71), 0),
    }


self_score = -100000.0
masked_score = -1000000000.0
norm_eps = 1e-06

def head_weights(query_rows, key_rows, inverse_norm, query_pos, key_pos):
    dots = jnp.dot(query_rows, key_rows.T, preferred_element_type=jnp.float32)
    raw_score = dots * inverse_norm[None, :]
    earlier = key_pos[None, :] < query_pos[:, None]
    itself = key_pos[None, :] == query_pos[:, None]
    score = jnp.where(earlier, raw_score, jnp.where(itself, jnp.float32(self_score), jnp.float32(masked_score)))
    top_score = lax.optimization_barrier(jnp.max(score, axis=1, keepdims=True))
    expo = jnp.exp(score - top_score)
    weights = expo / lax.optimization_barrier(jnp.sum(expo, axis=1, keepdims=True))
    return (raw_score, weights)

def head_output(weights, value_keys):
    weight_bf = weights.astype(jnp.bfloat16)
    output_rows = jnp.dot(weight_bf, value_keys, preferred_element_type=jnp.float32).astype(jnp.bfloat16)
    return (weight_bf, output_rows)

def head_grads(raw_score, weights, weight_bf, query_rows, key_rows, value_keys, inverse_norm, grad_rows, output_rows):
    value_dots = jnp.dot(grad_rows, value_keys.T, preferred_element_type=jnp.float32)
    row_delta = lax.optimization_barrier(jnp.sum(grad_rows.astype(jnp.float32) * output_rows.astype(jnp.float32), axis=1, keepdims=True))
    dscore = weights * (value_dots - row_delta)
    score_grad = (dscore * inverse_norm[None, :]).astype(jnp.bfloat16)
    query_grad = jnp.dot(score_grad, key_rows, preferred_element_type=jnp.float32)
    scaled_sum = lax.optimization_barrier(jnp.sum(dscore * raw_score, axis=0))
    key_grad = jnp.dot(score_grad.T, query_rows, preferred_element_type=jnp.float32)
    key_grad = key_grad - (scaled_sum * inverse_norm * inverse_norm)[:, None] * key_rows.astype(jnp.float32)
    value_grad = jnp.dot(weight_bf.T, grad_rows, preferred_element_type=jnp.float32)
    return (query_grad, key_grad, value_grad)

def key_norms(key_rows):
    key_float = key_rows.astype(jnp.float32)
    return lax.rsqrt(lax.optimization_barrier(jnp.sum(key_float * key_float, axis=1)) + norm_eps)

def reference(shared_qk, value_rows, out_grad, bucket_order, inverse_order):
    group_count = bucket_order.shape[0]
    group_width = shared_qk.shape[1] // group_count
    heads_group = group_width // HEAD_DIM
    block_total = TOKENS // BLOCK
    attended_parts = []
    grad_q_parts = []
    grad_v_parts = []
    for group_at in range(group_count):
        first_col = group_at * group_width
        order_row = bucket_order[group_at]
        sorted_q = jnp.take(shared_qk[:, first_col:first_col + group_width], order_row, axis=0)
        sorted_v = jnp.take(value_rows[:, first_col:first_col + group_width], order_row, axis=0)
        sorted_g = jnp.take(out_grad[:, first_col:first_col + group_width], order_row, axis=0)

        def per_block(block_at):
            start_row = (block_at * BLOCK).astype(jnp.int32)
            prior_row = ((block_at + block_total - 1) % block_total * BLOCK).astype(jnp.int32)

            def rows_of(source, begin):
                return lax.dynamic_slice_in_dim(source, begin, BLOCK, 0)
            query_all = rows_of(sorted_q, start_row)
            key_all = jnp.concatenate([rows_of(sorted_q, prior_row), query_all], axis=0)
            value_all = jnp.concatenate([rows_of(sorted_v, prior_row), rows_of(sorted_v, start_row)], axis=0)
            grad_all = rows_of(sorted_g, start_row)
            query_pos = rows_of(order_row, start_row)
            key_pos = jnp.concatenate([rows_of(order_row, prior_row), query_pos], axis=0)
            out_list, dq_list, dk_list, dv_list = ([], [], [], [])
            for head_at in range(heads_group):
                cols = slice(head_at * HEAD_DIM, (head_at + 1) * HEAD_DIM)
                query_rows = query_all[:, cols]
                key_rows = key_all[:, cols]
                value_keys = value_all[:, cols]
                inverse_norm = key_norms(key_rows)
                raw_score, weights = head_weights(query_rows, key_rows, inverse_norm, query_pos, key_pos)
                weight_bf, output_rows = head_output(weights, value_keys)
                query_grad, key_grad, value_grad = head_grads(raw_score, weights, weight_bf, query_rows, key_rows, value_keys, inverse_norm, grad_all[:, cols], output_rows)
                out_list.append(output_rows)
                dq_list.append(query_grad)
                dk_list.append(key_grad)
                dv_list.append(value_grad)
            return (jnp.concatenate(out_list, axis=1), jnp.concatenate(dq_list, axis=1), jnp.concatenate(dk_list, axis=1), jnp.concatenate(dv_list, axis=1))
        out_blocks, dq_blocks, dk_blocks, dv_blocks = lax.map(per_block, jnp.arange(block_total, dtype=jnp.int32))
        dk_total = dk_blocks[:, BLOCK:] + jnp.roll(dk_blocks[:, :BLOCK], -1, axis=0)
        dv_total = dv_blocks[:, BLOCK:] + jnp.roll(dv_blocks[:, :BLOCK], -1, axis=0)
        grad_q_sorted = (dq_blocks + dk_total).reshape(TOKENS, group_width).astype(jnp.bfloat16)
        grad_v_sorted = dv_total.reshape(TOKENS, group_width).astype(jnp.bfloat16)
        out_sorted = out_blocks.reshape(TOKENS, group_width)
        inverse_row = inverse_order[group_at]
        attended_parts.append(jnp.take(out_sorted, inverse_row, axis=0))
        grad_q_parts.append(jnp.take(grad_q_sorted, inverse_row, axis=0))
        grad_v_parts.append(jnp.take(grad_v_sorted, inverse_row, axis=0))
    return (jnp.concatenate(attended_parts, axis=1), jnp.concatenate(grad_q_parts, axis=1), jnp.concatenate(grad_v_parts, axis=1))
```

```python
import jax
import jax.numpy as jnp
from jax import lax
from jax.experimental import pallas as pl
from jax.experimental.pallas import tpu as pltpu
from jax.sharding import PartitionSpec as P

HEAD_DIM = 64
BLOCK = 512
RANKS = 6
PEERS = 128
CHIPS = 64
ROWS = 24
TILE = 128

log2_e = 1.4426950408889634
self_score = -100000.0 * log2_e
masked_score = -1000000000.0 * log2_e
norm_eps = 1e-06

F32 = jnp.float32
BF16 = jnp.bfloat16
I32 = jnp.int32


def iota(shape, dim):
    return lax.broadcasted_iota(I32, shape, dim)


def mm(a, b):
    return jnp.dot(a, b, preferred_element_type=F32)


def ones_where(mask):
    return jnp.where(mask, F32(1), F32(0)).astype(BF16)


def column(row):
    return jnp.transpose(jnp.broadcast_to(row.astype(F32), (128, row.shape[1])))


def lanes_equal(index_col, width):
    lane = iota(index_col.shape, 1)
    return jnp.concatenate(
        [ones_where(index_col == lane + 128 * n) for n in range(width // 128)], axis=1
    )


def rows_equal(index_row, height):
    return ones_where(iota((height, index_row.shape[1]), 0) == index_row)


def pack_kernel(slot_ref, order_ref, q_ref, v_ref, g_ref, msg_ref, code_ref, order_out_ref):
    order_out_ref[...] = order_ref[...]
    block = slot_ref[...] >> 9
    local = block.shape[1]
    member = iota((PEERS, local), 0) == block
    before = ones_where(iota((local, local), 0) < iota((local, local), 1))
    counts = mm(ones_where(member), before)
    rank = jnp.sum(jnp.where(member, counts, F32(0)), axis=0, keepdims=True)
    code = block * 8 + rank.astype(I32)
    code_ref[...] = code

    def wanted(first, count):
        shape = (CHIPS, count, 128)
        base = 16 * iota(shape, 0)
        at = iota(shape, 1) + first
        prior = base - 8 + at
        prior = jnp.where(prior < 0, prior + 8 * PEERS, prior)
        qv = jnp.where(at < 6, prior, jnp.where(at < 12, base + at - 6, base + at - 4))
        ga = jnp.where(at >= 18, base + at - 18, -1)
        gb = jnp.where(at >= 18, base + at - 10, -1)
        qv = jnp.where(at < 18, qv, -1)
        return [x.reshape(CHIPS * count, 128) for x in (qv, ga, gb)]

    def choose(want):
        return jnp.concatenate(
            [ones_where(want == code[:, 128 * n : 128 * n + 128]) for n in range(local // 128)],
            axis=1,
        )

    q, v, g = q_ref[...], v_ref[...], g_ref[...]
    h0, h1 = slice(0, HEAD_DIM), slice(HEAD_DIM, 2 * HEAD_DIM)
    none = jnp.zeros((local, HEAD_DIM), BF16)
    qv = jnp.concatenate([q[:, h0], v[:, h0], q[:, h1], v[:, h1]], axis=1)
    ga = jnp.concatenate([g[:, h0], none, g[:, h1], none], axis=1)
    gb = jnp.concatenate([none, g[:, h0], none, g[:, h1]], axis=1)
    head = mm(choose(wanted(0, 16)[0]), qv)
    pick = jnp.concatenate([choose(w) for w in wanted(16, 8)], axis=1)
    tail = mm(pick, jnp.concatenate([qv, ga, gb], axis=0))
    for c in range(2):
        cols = slice(128 * c, 128 * c + 128)
        rows = jnp.concatenate(
            [head[:, cols].reshape(CHIPS, 16, 128), tail[:, cols].reshape(CHIPS, 8, 128)], axis=1
        )
        msg_ref[:, c] = rows.astype(BF16)


def meta_kernel(z_ref, a_ref, b_ref, code_ref, rows_ref, cols_ref):
    n = BLOCK
    lane = iota((n, n), 1)
    at = iota((1, n), 1)

    def wide(col):
        return jnp.concatenate([col] * (n // 128), axis=1)

    for i, ref in enumerate((z_ref, a_ref, b_ref)):
        pos = ref[...].astype(F32)
        pos_col = wide(column(pos))
        place = jnp.sum(jnp.where(pos_col < pos, F32(1), F32(0)), axis=0, keepdims=True)
        place_col = wide(column(place)).astype(I32)
        ordered = jnp.sum(jnp.where(place_col == lane, pos_col, F32(0)), axis=0, keepdims=True)
        ordered_col = column(ordered)
        source = ordered.astype(I32) >> 9
        start = (source << 9).astype(F32)
        offset = jnp.sum(
            jnp.where(wide(ordered_col) < start, F32(1), F32(0)), axis=0, keepdims=True
        )
        code = source * 8 + at - offset.astype(I32)
        rows_ref[i : i + 1] = ordered.astype(I32)
        rows_ref[i + 3 : i + 4] = code
        if i > 0:
            cols_ref[i - 1] = ordered_col.astype(I32)
        cols_ref[i + 2] = column(code).astype(I32)
    rows_ref[6:8] = jnp.zeros((2, n), I32)
    cols_ref[5] = column(code_ref[...]).astype(I32)


def attend_kernel(arr_ref, rows_ref, cols_ref, out_ref, p_ref, ds_ref):
    n = BLOCK
    arrived = arr_ref[...].astype(F32)
    part = [
        arrived[:, 8 * i : 8 * i + 8].reshape(8 * PEERS, 128).astype(BF16) for i in range(3)
    ]
    part01 = jnp.concatenate(part[:2], axis=0)
    part12 = jnp.concatenate(part[1:], axis=0)
    group = 8 * PEERS

    def place_a(code):
        return jnp.where((code & 7) < 2, code + 6, group + code - 2)

    def place_b(code):
        return jnp.where((code & 7) < 4, code + 4, group + code - 4)

    code_z, code_a, code_b = cols_ref[2], cols_ref[3], cols_ref[4]
    x_z = mm(lanes_equal(code_z, group), part[0])
    x_a = mm(lanes_equal(place_a(code_a), 2 * group), part01)
    x_b = mm(lanes_equal(place_b(code_b), 2 * group), part12)
    g_a = mm(lanes_equal(code_a + 2, group), part[2])[:, :HEAD_DIM]
    g_b = mm(lanes_equal(code_b + 2, group), part[2])[:, HEAD_DIM:]

    ones = jnp.ones((n, HEAD_DIM), F32)

    def block_of(x):
        turned = jnp.transpose(x)
        q_t, v_t = turned[:HEAD_DIM], turned[HEAD_DIM:]
        norm = lax.rsqrt(jnp.sum(q_t * q_t, axis=0, keepdims=True) + norm_eps)
        q = x[:, :HEAD_DIM]
        norm_col = lax.rsqrt(jnp.sum(q * q, axis=1, keepdims=True) + norm_eps)
        return dict(
            q=q.astype(BF16),
            q_t=q_t,
            q_tb=q_t.astype(BF16),
            v_tb=v_t.astype(BF16),
            norm=norm,
            scale=norm * log2_e,
            key=(q * norm_col).astype(BF16),
            ones_v=jnp.concatenate([ones, x[:, HEAD_DIM:]], axis=1).astype(BF16),
        )

    blocks = [block_of(x) for x in (x_z, x_a, x_b)]

    def item(prior, own, grads, prior_pos, own_pos):
        outs, query_grads, scaled_grads = [], [], []
        for t in range(n // TILE):
            lo, hi = t * TILE, (t + 1) * TILE
            q = own["q"][lo:hi]
            s_prior = mm(q, prior["q_tb"]) * prior["scale"]
            pos_col = jnp.concatenate([own_pos[lo:hi]] * (n // 128), axis=1)
            s_prior = jnp.where(prior_pos < pos_col, s_prior, masked_score)
            s_own = mm(q, own["q_tb"][:, :hi]) * own["scale"][:, :hi]
            row, col = iota((TILE, TILE), 0), iota((TILE, TILE), 1)
            last = jnp.where(
                col < row, s_own[:, lo:], jnp.where(col == row, self_score, masked_score)
            )
            s_own = jnp.concatenate([s_own[:, :lo], last], axis=1) if t else last
            top = jnp.maximum(
                jnp.max(s_prior, axis=1, keepdims=True), jnp.max(s_own, axis=1, keepdims=True)
            )
            p_prior = jnp.exp2(s_prior - top)
            p_own = jnp.exp2(s_own - top)
            pb_prior, pb_own = p_prior.astype(BF16), p_own.astype(BF16)
            summed = mm(pb_prior, prior["ones_v"]) + mm(pb_own, own["ones_v"][:hi])
            inverse = 1.0 / summed[:, :HEAD_DIM]
            out = (summed[:, HEAD_DIM:] * inverse).astype(BF16)
            grad = (grads[lo:hi] * inverse).astype(BF16)
            delta = jnp.sum(grad.astype(F32) * out.astype(F32), axis=1, keepdims=True)
            ds_prior = (p_prior * (mm(grad, prior["v_tb"]) - delta)).astype(BF16)
            ds_own = (p_own * (mm(grad, own["v_tb"][:, :hi]) - delta)).astype(BF16)
            query_grads.append(mm(ds_prior, prior["key"]) + mm(ds_own, own["key"][:hi]))
            outs.append(out)
            scaled_grads.append(grad)
            p_ref[lo:hi, :n] = pb_prior
            ds_ref[lo:hi, :n] = ds_prior
            p_ref[lo:hi, n : n + hi] = pb_own
            ds_ref[lo:hi, n : n + hi] = ds_own
            if hi < n:
                rest = jnp.zeros((TILE, n - hi), BF16)
                p_ref[lo:hi, n + hi :] = rest
                ds_ref[lo:hi, n + hi :] = rest
        grad_t = jnp.transpose(jnp.concatenate(scaled_grads, axis=0).astype(F32)).astype(BF16)
        half = n // 2

        def back(left, ref):
            whole = mm(left, ref[:, : n + half])
            late = mm(left[:, half:], ref[half:, n + half :])
            return whole[:, :n], jnp.concatenate([whole[:, n:], late], axis=1)

        dk_prior, dk_own = back(own["q_tb"], ds_ref)
        dv_prior, dv_own = back(grad_t, p_ref)
        return (
            jnp.concatenate(outs, axis=0),
            jnp.concatenate(query_grads, axis=0),
            (dk_prior, dv_prior),
            (dk_own, dv_own),
        )

    block_z, block_a, block_b = blocks
    pos_z, pos_a = rows_ref[0:1], rows_ref[1:2]
    out_a, dq_a, sums_z, sums_a = item(block_z, block_a, g_a, pos_z, cols_ref[0])
    out_b, dq_b, more_a, sums_b = item(block_a, block_b, g_b, pos_a, cols_ref[1])
    sums_a = (sums_a[0] + more_a[0], sums_a[1] + more_a[1])

    def result(block, sums, query_grad):
        dk, dv = sums
        norm, q_t = block["norm"], block["q_t"]
        along = jnp.sum(q_t * dk, axis=0, keepdims=True) * (norm * norm)
        dk = norm * (dk - along * q_t)
        both = jnp.transpose(jnp.concatenate([dk, dv], axis=0))
        if query_grad is not None:
            both = jnp.concatenate(
                [both[:, :HEAD_DIM] + query_grad, both[:, HEAD_DIM:]], axis=1
            )
        return both.astype(BF16)

    r_z = result(block_z, sums_z, None)
    r_a = result(block_a, sums_a, dq_a)
    r_b = result(block_b, sums_b, dq_b)
    none = jnp.zeros((n, HEAD_DIM), BF16)
    o_a = jnp.concatenate([out_a, none], axis=1)
    o_b = jnp.concatenate([none, out_b], axis=1)

    row_z, row_a, row_b = rows_ref[3:4], rows_ref[4:5], rows_ref[5:6]
    at_a, at_b = place_a(row_a), place_b(row_b)

    def send(places, values):
        chosen = jnp.concatenate([rows_equal(at, group) for at in places], axis=1)
        return mm(chosen, jnp.concatenate(values, axis=0)).reshape(PEERS, 8, 128)

    sent = [
        send([row_z, at_a], [r_z, r_a]),
        send([at_a - group, at_b], [r_a, r_b]),
        send([at_b - group, row_a + 2, row_b + 2], [r_b, o_a, o_b]),
    ]
    out_ref[...] = jnp.concatenate(sent, axis=1).astype(BF16)


def restore_kernel(ret_ref, code_ref, att_ref, dqk_ref, dv_ref):
    code = code_ref[0]
    block, rank = code >> 3, code & 7
    chip, odd = block >> 1, (block & 1) == 1
    group = 8 * CHIPS
    base = chip * 8 + rank
    even_at = jnp.where(rank < 2, base + 6, group + base - 2)
    odd_at = jnp.where(rank < 4, group + base + 4, 2 * group + base - 4)
    own_at = jnp.where(odd, odd_at, even_at)
    prior_at = jnp.where(odd, ((chip + 1) & (CHIPS - 1)) * 8 + rank, -1)
    lane = iota(code.shape, 1)
    chosen = jnp.concatenate(
        [
            ones_where((own_at == lane + 128 * i) | (prior_at == lane + 128 * i))
            for i in range(3 * group // 128)
        ],
        axis=1,
    )
    returned = ret_ref[...].astype(F32)
    values = [
        jnp.concatenate(
            [returned[:, c, 8 * i : 8 * i + 8].reshape(group, 128) for c in range(2)], axis=1
        ).astype(BF16)
        for i in range(3)
    ]
    grads = mm(chosen, jnp.concatenate(values, axis=0)).astype(BF16)
    outs = mm(lanes_equal(base + 2, group), values[2])
    h = HEAD_DIM
    odd_h = odd[:, :h]
    att_ref[...] = jnp.concatenate(
        [
            jnp.where(odd_h, outs[:, h : 2 * h], outs[:, :h]),
            jnp.where(odd_h, outs[:, 3 * h :], outs[:, 2 * h : 3 * h]),
        ],
        axis=1,
    ).astype(BF16)
    dqk_ref[...] = jnp.concatenate([grads[:, :h], grads[:, 2 * h : 3 * h]], axis=1)
    dv_ref[...] = jnp.concatenate([grads[:, h : 2 * h], grads[:, 3 * h :]], axis=1)


def struct(shape, dtype):
    return jax.ShapeDtypeStruct(shape, dtype)


def params(mib):
    return pltpu.CompilerParams(vmem_limit_bytes=mib * 1024 * 1024)


def pack(slots, order, q, v, g):
    n = q.shape[0]
    return pl.pallas_call(
        pack_kernel,
        out_shape=(
            struct((CHIPS, 2, ROWS, 128), BF16),
            struct((1, n), I32),
            struct((1, n), I32),
        ),
        compiler_params=params(32),
        name="pack",
    )(slots, order, q, v, g)


def meta(z, a, b, code):
    return pl.pallas_call(
        meta_kernel,
        out_shape=(struct((8, BLOCK), I32), struct((6, BLOCK, 128), I32)),
        compiler_params=params(32),
        name="meta",
    )(z, a, b, code)


def attend(arrived, rows, cols):
    return pl.pallas_call(
        attend_kernel,
        out_shape=struct((PEERS, ROWS, 128), BF16),
        scratch_shapes=[pltpu.VMEM((BLOCK, 2 * BLOCK), BF16)] * 2,
        compiler_params=params(48),
        name="attend",
    )(arrived, rows, cols)


def restore(returned, cols):
    n = cols.shape[1]
    return pl.pallas_call(
        restore_kernel,
        grid=(1,),
        in_specs=[
            pl.BlockSpec((CHIPS, 2, ROWS, 128), lambda i: (0, 0, 0, 0)),
            pl.BlockSpec((1, n, 128), lambda i: (5, 0, 0)),
        ],
        out_specs=[pl.BlockSpec((n, 128), lambda i: (0, 0))] * 3,
        out_shape=[struct((n, 128), BF16)] * 3,
        compiler_params=params(32),
        name="restore",
    )(returned, cols)


def exchange(message):
    return lax.all_to_all(message, "seq", split_axis=0, concat_axis=0, tiled=True)


def per_device(shared_qk, value_rows, out_grad, bucket_order, inverse_order):
    message, code, order = pack(inverse_order, bucket_order, shared_qk, value_rows, out_grad)
    arrived = exchange(message.reshape(PEERS, ROWS, 128))
    peers = range(PEERS)
    other = lax.ppermute(order, "seq", [(i, i ^ 1) for i in peers])
    first = lax.axis_index("seq") % 2 == 0
    order_a = jnp.where(first, order, other)
    order_b = jnp.where(first, other, order)
    order_z = lax.ppermute(order_b, "seq", [(i, (i + 2) % PEERS) for i in peers])
    rows, cols = meta(order_z, order_a, order_b, code)
    returned = exchange(attend(arrived, rows, cols))
    attended, grad_qk, grad_v = restore(returned.reshape(CHIPS, 2, ROWS, 128), cols)
    return attended, grad_qk, grad_v


def solution(mesh):
    rows, orders = P("seq", "head"), P("head", "seq")
    return jax.shard_map(
        per_device,
        mesh=mesh,
        in_specs=(rows, rows, rows, orders, orders),
        out_specs=(rows, rows, rows),
        check_vma=False,
    )
```

```python
import jax
import jax.numpy as jnp
from jax import lax
from jax.experimental import pallas as pl
from jax.experimental.pallas import tpu as pltpu
from jax.sharding import PartitionSpec as P

HEAD_DIM = 64
BLOCK = 512
RANKS = 6
PEERS = 128
CHIPS = 64
ROWS = 24

META_FLOPS = 12 * 10**9

log2_e = 1.4426950408889634
self_score = -100000.0 * log2_e
masked_score = -1000000000.0 * log2_e
norm_eps = 1e-06

F32 = jnp.float32
BF16 = jnp.bfloat16
I32 = jnp.int32


def iota(shape, dim):
    return lax.broadcasted_iota(I32, shape, dim)


def mm(a, b):
    return jnp.dot(a, b, preferred_element_type=F32)


def ones_where(mask):
    return jnp.where(mask, F32(1), F32(0)).astype(BF16)


def column(row):
    return jnp.transpose(jnp.broadcast_to(row.astype(F32), (128, row.shape[1])))


def lanes_equal(index_col, width):
    lane = iota(index_col.shape, 1)
    return jnp.concatenate(
        [ones_where(index_col == lane + 128 * n) for n in range(width // 128)], axis=1
    )


def rows_equal(index_row, height):
    return ones_where(iota((height, index_row.shape[1]), 0) == index_row)


def tiles_of(rows):
    count = rows.shape[0] * 8
    mixed = jnp.concatenate(
        [rows[:, 6:8], rows[:, 14:16], rows[:, 22:24], jnp.zeros_like(rows[:, :2])], axis=1
    )
    tiles = [rows[:, 8 * i : 8 * i + 8] for i in range(3)] + [mixed]
    return [t.reshape(count, 128).astype(BF16) for t in tiles]


def rows_of(tiles, mixed):
    pieces = []
    for i, tile in enumerate(tiles):
        pieces += [tile[:, :6], mixed[:, 2 * i : 2 * i + 2]]
    return jnp.concatenate(pieces, axis=1).astype(BF16)


def pack_kernel(slot_hbm, q_hbm, v_hbm, g_hbm, msg_ref, code_ref, slot_ref, q_ref, v_ref, g_ref, sems):
    copies = [
        pltpu.make_async_copy(src, dst, sems.at[i])
        for i, (src, dst) in enumerate(
            [(slot_hbm, slot_ref), (q_hbm, q_ref), (v_hbm, v_ref), (g_hbm, g_ref)]
        )
    ]
    for copy in copies:
        copy.start()
    copies[0].wait()
    block = slot_ref[...] >> 9
    local = block.shape[1]
    member = iota((PEERS, local), 0) == block
    before = ones_where(iota((local, local), 0) < iota((local, local), 1))
    counts = mm(ones_where(member), before)
    rank = jnp.sum(jnp.where(member, counts, F32(0)), axis=0, keepdims=True)
    code = block * 8 + rank.astype(I32)
    code_ref[...] = code

    def choose(offset):
        shape = (CHIPS, 8, 128)
        want = 16 * iota(shape, 0) + iota(shape, 1) + offset
        want = jnp.where(want < 0, want + 8 * PEERS, want).reshape(CHIPS * 8, 128)
        return jnp.concatenate(
            [ones_where(want == code[:, 128 * n : 128 * n + 128]) for n in range(local // 128)],
            axis=1,
        )

    chosen = [choose(offset) for offset in (-8, 0, 8)]
    for copy in copies[1:]:
        copy.wait()
    q, v, g = q_ref[...], v_ref[...], g_ref[...]
    h0, h1 = slice(0, HEAD_DIM), slice(HEAD_DIM, 2 * HEAD_DIM)
    none = jnp.zeros((local, HEAD_DIM), BF16)
    qv = jnp.concatenate([q[:, h0], v[:, h0], q[:, h1], v[:, h1]], axis=1)
    ga = jnp.concatenate([g[:, h0], none, g[:, h1], none], axis=1)
    gb = jnp.concatenate([none, g[:, h0], none, g[:, h1]], axis=1)
    tiles = [mm(one, qv) for one in chosen]
    mixed = mm(jnp.concatenate(chosen[1:], axis=1), jnp.concatenate([ga, gb], axis=0))
    for c in range(2):
        cols = slice(128 * c, 128 * c + 128)
        msg_ref[:, c] = rows_of(
            [t[:, cols].reshape(CHIPS, 8, 128) for t in tiles],
            mixed[:, cols].reshape(CHIPS, 8, 128),
        )


def meta_kernel(orders_ref, code_ref, table_ref):
    n = BLOCK
    lane = iota((n, n), 1)
    at = iota((1, n), 1)

    def wide(col):
        return jnp.concatenate([col] * (n // 128), axis=1)

    for i in range(3):
        pos = orders_ref[i : i + 1].astype(F32)
        pos_col = wide(column(pos))
        place = jnp.sum(jnp.where(pos_col < pos, F32(1), F32(0)), axis=0, keepdims=True)
        place_col = wide(column(place)).astype(I32)
        ordered = jnp.sum(jnp.where(place_col == lane, pos_col, F32(0)), axis=0, keepdims=True)
        source = ordered.astype(I32) >> 9
        start = (source << 9).astype(F32)
        offset = jnp.sum(
            jnp.where(wide(column(ordered)) < start, F32(1), F32(0)), axis=0, keepdims=True
        )
        table_ref[i : i + 1] = ordered.astype(I32)
        table_ref[i + 3 : i + 4] = source * 8 + at - offset.astype(I32)
    table_ref[6:7] = code_ref[...]
    table_ref[7:8] = jnp.zeros((1, n), I32)


def nt(a, b):
    return lax.dot_general(a, b, (((1,), (1,)), ((), ())), preferred_element_type=F32)


def tn(a, b):
    return lax.dot_general(a, b, (((0,), (0,)), ((), ())), preferred_element_type=F32)


def two_terms(x):
    high = x.astype(BF16)
    return high, (x - high.astype(F32)).astype(BF16)


def attend_kernel(arr_ref, table_hbm, out_ref, give_ref, rows_ref, sem):
    n, half, group = BLOCK, BLOCK // 2, 8 * PEERS
    fetch = pltpu.make_async_copy(table_hbm, rows_ref, sem)
    fetch.start()
    part_z, part_a, part_b, part_g = tiles_of(arr_ref[...].astype(F32))
    fetch.wait()
    reach = 3 * group // 4

    def take(i, part):
        code = rows_ref[3 + i : 4 + i]
        first, last = slice(0, half), slice(half, n)
        give_ref[i, :reach, first] = rows_equal(code[:, first], reach)
        give_ref[i, group - reach :, last] = rows_equal(code[:, last] - (group - reach), reach)
        return jnp.concatenate(
            [
                tn(part[:reach], give_ref[i, :reach, first]),
                tn(part[group - reach :], give_ref[i, group - reach :, last]),
            ],
            axis=1,
        )

    x_z = take(0, part_z)
    x_a = take(1, jnp.concatenate([part_a, part_g], axis=1))
    x_b = take(2, jnp.concatenate([part_b, part_g], axis=1))
    h = HEAD_DIM
    g_a, g_b = x_a[2 * h : 3 * h], x_b[3 * h :]
    pad = jnp.zeros((14, n), BF16)
    ones = jnp.ones((16, n), BF16)

    def block_of(x):
        q, v = x[:h], x[h : 2 * h]
        norm = lax.rsqrt(jnp.sum(q * q, axis=0, keepdims=True) + norm_eps)
        return dict(
            q=q,
            qb=q.astype(BF16),
            vb=jnp.concatenate([v.astype(BF16), ones], axis=0),
            norm=norm,
            scale=norm * log2_e,
            key=(q * norm).astype(BF16),
        )

    block_z, block_a, block_b = [block_of(x) for x in (x_z, x_a, x_b)]

    def item(prior, own, grads, prior_pos, own_pos):
        pos = jnp.concatenate([column(own_pos)] * (n // 128), axis=1)
        s_prior = tn(own["qb"], prior["qb"]) * prior["scale"]
        s_prior = jnp.where(prior_pos.astype(F32) < pos, s_prior, masked_score)
        s_own = tn(own["qb"], own["qb"]) * own["scale"]
        row, col = iota((n, n), 0), iota((n, n), 1)
        s_own = jnp.where(col < row, s_own, jnp.where(col == row, self_score, masked_score))
        top = jnp.maximum(
            jnp.max(s_prior, axis=1, keepdims=True), jnp.max(s_own, axis=1, keepdims=True)
        )
        p_prior = jnp.exp2(s_prior - top)
        p_own = jnp.exp2(s_own - top)
        pb_prior, pb_own = p_prior.astype(BF16), p_own.astype(BF16)
        summed = nt(prior["vb"], pb_prior) + nt(own["vb"], pb_own)
        inverse = 1.0 / summed[h : h + 1]
        out = (summed[:h] * inverse).astype(BF16)
        grad = (grads * inverse).astype(BF16)
        delta = jnp.sum(grad.astype(F32) * out.astype(F32), axis=0, keepdims=True)
        left = jnp.concatenate([grad, *two_terms(-delta), pad], axis=0)
        ds_prior = (p_prior * tn(left, prior["vb"])).astype(BF16)
        ds_own = (p_own * tn(left, own["vb"])).astype(BF16)
        dq = nt(prior["key"], ds_prior) + nt(own["key"], ds_own)
        sums_prior = (mm(own["qb"], ds_prior), mm(grad, pb_prior))
        sums_own = (mm(own["qb"], ds_own), mm(grad, pb_own))
        return out, dq, sums_prior, sums_own

    pos_z, pos_a, pos_b = rows_ref[0:1], rows_ref[1:2], rows_ref[2:3]
    out_a, dq_a, sums_z, sums_a = item(block_z, block_a, g_a, pos_z, pos_a)
    out_b, dq_b, more_a, sums_b = item(block_a, block_b, g_b, pos_a, pos_b)
    sums_a = (sums_a[0] + more_a[0], sums_a[1] + more_a[1])

    def result(block, sums, query_grad):
        dk, dv = sums
        norm, q = block["norm"], block["q"]
        along = jnp.sum(q * dk, axis=0, keepdims=True) * (norm * norm)
        dk = norm * (dk - along * q)
        if query_grad is not None:
            dk = dk + query_grad
        return [dk.astype(BF16), dv.astype(BF16)]

    def send(i, pieces):
        turned = jnp.concatenate(pieces, axis=0)
        sent = []
        for t, (lo, hi) in enumerate([(0, half), (0, n), (0, n), (half, n)]):
            sent.append(nt(give_ref[i, t * group // 4 : (t + 1) * group // 4, lo:hi], turned[:, lo:hi]))
        return jnp.concatenate(sent, axis=0)

    give_ref[:, reach:, :half] = jnp.zeros((3, group - reach, half), BF16)
    give_ref[:, : group - reach, half:] = jnp.zeros((3, group - reach, half), BF16)
    none = jnp.zeros((h, n), BF16)
    s_z = send(0, result(block_z, sums_z, None)).reshape(PEERS, 8, 128)
    s_a = send(1, [*result(block_a, sums_a, dq_a), out_a, none])
    s_b = send(2, [*result(block_b, sums_b, dq_b), none, out_b])
    mixed = (s_a[:, 128:] + s_b[:, 128:]).reshape(PEERS, 8, 128)
    s_a, s_b = (s[:, :128].reshape(PEERS, 8, 128) for s in (s_a, s_b))
    out_ref[...] = rows_of([s_z, s_a, s_b], mixed)


def restore_kernel(ret_ref, code_ref, att_ref, dqk_ref, dv_ref):
    code = column(code_ref[...]).astype(I32)
    block, rank = code >> 3, code & 7
    chip, odd = block >> 1, (block & 1) == 1
    group = 8 * CHIPS
    own_at = chip * 8 + rank
    prior_at = jnp.where(odd, ((chip + 1) & (CHIPS - 1)) * 8 + rank, -1)
    chosen = jnp.concatenate(
        [
            lanes_equal(prior_at, group),
            lanes_equal(jnp.where(odd, -1, own_at), group),
            lanes_equal(jnp.where(odd, own_at, -1), group),
        ],
        axis=1,
    )
    tiles = [tiles_of(ret_ref[:, c].astype(F32)) for c in range(2)]
    values = [jnp.concatenate([t[i] for t in tiles], axis=1) for i in range(4)]
    grads = mm(chosen, jnp.concatenate(values[:3], axis=0)).astype(BF16)
    outs = mm(lanes_equal(own_at, group), values[3])
    h = HEAD_DIM
    odd_h = odd[:, :h]
    att_ref[...] = jnp.concatenate(
        [
            jnp.where(odd_h, outs[:, h : 2 * h], outs[:, :h]),
            jnp.where(odd_h, outs[:, 3 * h :], outs[:, 2 * h : 3 * h]),
        ],
        axis=1,
    ).astype(BF16)
    dqk_ref[...] = jnp.concatenate([grads[:, :h], grads[:, 2 * h : 3 * h]], axis=1)
    dv_ref[...] = jnp.concatenate([grads[:, h : 2 * h], grads[:, 3 * h :]], axis=1)


def struct(shape, dtype):
    return jax.ShapeDtypeStruct(shape, dtype)


def params(mib):
    return pltpu.CompilerParams(vmem_limit_bytes=mib * 1024 * 1024)


def in_hbm(x):
    return pltpu.with_memory_space_constraint(x, pltpu.HBM)


def pack(slots, q, v, g):
    n = q.shape[0]
    return pl.pallas_call(
        pack_kernel,
        in_specs=[pl.BlockSpec(memory_space=pltpu.HBM)] * 4,
        out_shape=(struct((CHIPS, 2, ROWS, 128), BF16), struct((1, n), I32)),
        scratch_shapes=[pltpu.VMEM((1, n), I32)]
        + [pltpu.VMEM((n, 128), BF16)] * 3
        + [pltpu.SemaphoreType.DMA((4,))],
        compiler_params=params(24),
        name="pack",
    )(*map(in_hbm, (slots, q, v, g)))


def meta(orders, code):
    return pl.pallas_call(
        meta_kernel,
        out_shape=struct((8, BLOCK), I32),
        compiler_params=params(24),
        cost_estimate=pl.CostEstimate(
            flops=META_FLOPS, bytes_accessed=32768, transcendentals=0
        ),
        name="meta",
    )(orders, code)


def attend(arrived, table):
    return pl.pallas_call(
        attend_kernel,
        in_specs=[pl.BlockSpec(memory_space=pltpu.VMEM), pl.BlockSpec(memory_space=pltpu.HBM)],
        out_shape=struct((PEERS, ROWS, 128), BF16),
        scratch_shapes=[
            pltpu.VMEM((3, 8 * PEERS, BLOCK), BF16),
            pltpu.VMEM((8, BLOCK), I32),
            pltpu.SemaphoreType.DMA(()),
        ],
        compiler_params=params(40),
        name="attend",
    )(arrived, in_hbm(table))


def restore(returned, code):
    n = code.shape[1]
    return pl.pallas_call(
        restore_kernel,
        out_shape=[struct((n, 128), BF16)] * 3,
        compiler_params=params(24),
        name="restore",
    )(returned, code)


def exchange(message):
    return lax.all_to_all(message, "seq", split_axis=0, concat_axis=0, tiled=True)


def per_device(shared_qk, value_rows, out_grad, bucket_order, inverse_order):
    peers = range(PEERS)
    before = lax.ppermute(bucket_order, "seq", [(i, (i + 2) % PEERS) for i in peers])
    held = jnp.concatenate([bucket_order, before], axis=0)
    other = lax.ppermute(held, "seq", [(i, i ^ 1) for i in peers])
    even = lax.axis_index("seq") & 1 == 0
    near = jnp.concatenate(
        [
            jnp.where(even, other[1:], before),
            jnp.where(even, bucket_order, other[:1]),
            jnp.where(even, other[:1], bucket_order),
        ],
        axis=0,
    )
    message, code = pack(inverse_order, shared_qk, value_rows, out_grad)
    arrived = exchange(message.reshape(PEERS, ROWS, 128))
    returned = exchange(attend(arrived, meta(near, code)))
    return tuple(restore(returned.reshape(CHIPS, 2, ROWS, 128), code))


def solution(mesh):
    rows, orders = P("seq", "head"), P("head", "seq")
    return jax.shard_map(
        per_device,
        mesh=mesh,
        in_specs=(rows, rows, rows, orders, orders),
        out_specs=(rows, rows, rows),
        check_vma=False,
    )
```

```python
import jax
import jax.numpy as jnp
from jax import lax
from jax.experimental import pallas as pl
from jax.experimental.pallas import tpu as pltpu
from jax.sharding import PartitionSpec as P

HEAD_DIM = 64
BLOCK = 512
RANKS = 6
PEERS = 128
CHIPS = 64
ROWS = 24

META_FLOPS = 12 * 10**9

log2_e = 1.4426950408889634
self_score = -100000.0 * log2_e
masked_score = -1000000000.0 * log2_e
norm_eps = 1e-06

F32 = jnp.float32
BF16 = jnp.bfloat16
I32 = jnp.int32


def iota(shape, dim):
    return lax.broadcasted_iota(I32, shape, dim)


def mm(a, b):
    return jnp.dot(a, b, preferred_element_type=F32)


def ones_where(mask):
    return jnp.where(mask, F32(1), F32(0)).astype(BF16)


def column(row):
    return jnp.transpose(jnp.broadcast_to(row.astype(F32), (128, row.shape[1])))


def lanes_equal(index_col, width):
    lane = iota(index_col.shape, 1)
    return jnp.concatenate(
        [ones_where(index_col == lane + 128 * n) for n in range(width // 128)], axis=1
    )


def rows_equal(index_row, height):
    return ones_where(iota((height, index_row.shape[1]), 0) == index_row)


def tiles_of(rows):
    count = rows.shape[0] * 8
    mixed = jnp.concatenate(
        [rows[:, 6:8], rows[:, 14:16], rows[:, 22:24], jnp.zeros_like(rows[:, :2])], axis=1
    )
    tiles = [rows[:, 8 * i : 8 * i + 8] for i in range(3)] + [mixed]
    return [t.reshape(count, 128).astype(BF16) for t in tiles]


def rows_of(tiles, mixed):
    pieces = []
    for i, tile in enumerate(tiles):
        pieces += [tile[:, :6], mixed[:, 2 * i : 2 * i + 2]]
    return jnp.concatenate(pieces, axis=1).astype(BF16)


def pack_kernel(slot_hbm, q_hbm, v_hbm, g_hbm, msg_ref, code_ref, slot_ref, q_ref, v_ref, g_ref, sems):
    copies = [
        pltpu.make_async_copy(src, dst, sems.at[i])
        for i, (src, dst) in enumerate(
            [(slot_hbm, slot_ref), (q_hbm, q_ref), (v_hbm, v_ref), (g_hbm, g_ref)]
        )
    ]
    for copy in copies:
        copy.start()
    copies[0].wait()
    block = slot_ref[...] >> 9
    local = block.shape[1]
    member = iota((PEERS, local), 0) == block
    before = ones_where(iota((local, local), 0) < iota((local, local), 1))
    counts = mm(ones_where(member), before)
    rank = jnp.sum(jnp.where(member, counts, F32(0)), axis=0, keepdims=True)
    code = block * 8 + rank.astype(I32)
    code_ref[...] = code

    def choose(offset):
        shape = (CHIPS, 8, 128)
        want = 16 * iota(shape, 0) + iota(shape, 1) + offset
        want = jnp.where(want < 0, want + 8 * PEERS, want).reshape(CHIPS * 8, 128)
        return jnp.concatenate(
            [ones_where(want == code[:, 128 * n : 128 * n + 128]) for n in range(local // 128)],
            axis=1,
        )

    chosen = [choose(offset) for offset in (-8, 0, 8)]
    for copy in copies[1:]:
        copy.wait()
    q, v, g = q_ref[...], v_ref[...], g_ref[...]
    h0, h1 = slice(0, HEAD_DIM), slice(HEAD_DIM, 2 * HEAD_DIM)
    none = jnp.zeros((local, HEAD_DIM), BF16)
    qv = jnp.concatenate([q[:, h0], v[:, h0], q[:, h1], v[:, h1]], axis=1)
    ga = jnp.concatenate([g[:, h0], none, g[:, h1], none], axis=1)
    gb = jnp.concatenate([none, g[:, h0], none, g[:, h1]], axis=1)
    tiles = [mm(one, qv) for one in chosen]
    mixed = mm(jnp.concatenate(chosen[1:], axis=1), jnp.concatenate([ga, gb], axis=0))
    for c in range(2):
        cols = slice(128 * c, 128 * c + 128)
        msg_ref[:, c] = rows_of(
            [t[:, cols].reshape(CHIPS, 8, 128) for t in tiles],
            mixed[:, cols].reshape(CHIPS, 8, 128),
        )


def meta_kernel(orders_ref, code_ref, table_ref):
    n = BLOCK
    lane = iota((n, n), 1)
    at = iota((1, n), 1)

    def wide(col):
        return jnp.concatenate([col] * (n // 128), axis=1)

    for i in range(3):
        pos = orders_ref[i : i + 1].astype(F32)
        pos_col = wide(column(pos))
        place = jnp.sum(jnp.where(pos_col < pos, F32(1), F32(0)), axis=0, keepdims=True)
        place_col = wide(column(place)).astype(I32)
        ordered = jnp.sum(jnp.where(place_col == lane, pos_col, F32(0)), axis=0, keepdims=True)
        source = ordered.astype(I32) >> 9
        start = (source << 9).astype(F32)
        offset = jnp.sum(
            jnp.where(wide(column(ordered)) < start, F32(1), F32(0)), axis=0, keepdims=True
        )
        table_ref[i : i + 1] = ordered.astype(I32)
        table_ref[i + 3 : i + 4] = source * 8 + at - offset.astype(I32)
    table_ref[6:7] = code_ref[...]
    table_ref[7:8] = jnp.zeros((1, n), I32)


def nt(a, b):
    return lax.dot_general(a, b, (((1,), (1,)), ((), ())), preferred_element_type=F32)


def tn(a, b):
    return lax.dot_general(a, b, (((0,), (0,)), ((), ())), preferred_element_type=F32)


def two_terms(x):
    high = x.astype(BF16)
    return high, (x - high.astype(F32)).astype(BF16)


def attend_kernel(arr_ref, rows_ref, out_hbm, give_ref, out_ref, sems):
    n, half, group = BLOCK, BLOCK // 2, 8 * PEERS
    part_z, part_a, part_b, part_g = tiles_of(arr_ref[...].astype(F32))
    reach = 3 * group // 4

    def take(i, part):
        code = rows_ref[3 + i : 4 + i]
        first, last = slice(0, half), slice(half, n)
        give_ref[i, :reach, first] = rows_equal(code[:, first], reach)
        give_ref[i, group - reach :, last] = rows_equal(code[:, last] - (group - reach), reach)
        return jnp.concatenate(
            [
                tn(part[:reach], give_ref[i, :reach, first]),
                tn(part[group - reach :], give_ref[i, group - reach :, last]),
            ],
            axis=1,
        )

    give_ref[:, reach:, :half] = jnp.zeros((3, group - reach, half), BF16)
    give_ref[:, : group - reach, half:] = jnp.zeros((3, group - reach, half), BF16)
    x_z = take(0, part_z)
    x_a = take(1, jnp.concatenate([part_a, part_g], axis=1))
    x_b = take(2, jnp.concatenate([part_b, part_g], axis=1))
    h = HEAD_DIM
    g_a, g_b = x_a[2 * h : 3 * h], x_b[3 * h :]
    pad = jnp.zeros((14, n), BF16)
    ones = jnp.ones((16, n), BF16)

    def block_of(x):
        q, v = x[:h], x[h : 2 * h]
        norm = lax.rsqrt(jnp.sum(q * q, axis=0, keepdims=True) + norm_eps)
        return dict(
            q=q,
            qb=q.astype(BF16),
            vb=jnp.concatenate([v.astype(BF16), ones], axis=0),
            norm=norm,
            scale=norm * log2_e,
            key=(q * norm).astype(BF16),
        )

    block_z, block_a, block_b = [block_of(x) for x in (x_z, x_a, x_b)]

    first, last = slice(0, half), slice(half, n)
    row, col = iota((half, half), 0), iota((half, half), 1)

    def low_high(x):
        return x[:half], x[half:]

    def late(x, y):
        return jnp.concatenate([x[:, first], x[:, last] + y], axis=1)

    def item(prior, own, grads, prior_pos, own_pos):
        q = own["qb"]
        pos = jnp.concatenate([column(own_pos)] * (n // 128), axis=1)
        s0 = tn(q, prior["qb"]) * prior["scale"]
        s0 = jnp.where(prior_pos.astype(F32) < pos, s0, masked_score)
        s1 = tn(q, own["qb"][:, first]) * own["scale"][:, first]
        s2 = tn(q[:, last], own["qb"][:, last]) * own["scale"][:, last]

        def triangle(s):
            return jnp.where(col < row, s, jnp.where(col == row, self_score, masked_score))

        s1 = jnp.concatenate([triangle(s1[:half]), s1[half:]], axis=0)
        s2 = triangle(s2)
        top0, top1, top2 = (jnp.max(s, axis=1, keepdims=True) for s in (s0, s1, s2))
        top_low, top_high = low_high(jnp.maximum(top0, top1))
        top_high = jnp.maximum(top_high, top2)
        top = jnp.concatenate([top_low, top_high], axis=0)
        p0, p1, p2 = jnp.exp2(s0 - top), jnp.exp2(s1 - top), jnp.exp2(s2 - top_high)
        b0, b1, b2 = p0.astype(BF16), p1.astype(BF16), p2.astype(BF16)
        v0, v1, v2 = prior["vb"], own["vb"][:, first], own["vb"][:, last]
        summed = late(nt(v0, b0) + nt(v1, b1), nt(v2, b2))
        inverse = 1.0 / summed[h : h + 1]
        out = (summed[:h] * inverse).astype(BF16)
        grad = (grads * inverse).astype(BF16)
        delta = jnp.sum(grad.astype(F32) * out.astype(F32), axis=0, keepdims=True)
        left = jnp.concatenate([grad, *two_terms(-delta), pad], axis=0)
        d0 = (p0 * tn(left, v0)).astype(BF16)
        d1 = (p1 * tn(left, v1)).astype(BF16)
        d2 = (p2 * tn(left[:, last], v2)).astype(BF16)
        dq = late(
            nt(prior["key"], d0) + nt(own["key"][:, first], d1), nt(own["key"][:, last], d2)
        )
        sums_prior = (mm(q, d0), mm(grad, b0))
        sums_own = tuple(
            jnp.concatenate([mm(x, lo), mm(x[:, last], hi)], axis=1)
            for x, lo, hi in ((q, d1, d2), (grad, b1, b2))
        )
        return out, dq, sums_prior, sums_own

    pos_z, pos_a, pos_b = rows_ref[0:1], rows_ref[1:2], rows_ref[2:3]
    out_a, dq_a, sums_z, sums_a = item(block_z, block_a, g_a, pos_z, pos_a)
    out_b, dq_b, more_a, sums_b = item(block_a, block_b, g_b, pos_a, pos_b)
    sums_a = (sums_a[0] + more_a[0], sums_a[1] + more_a[1])

    def result(block, sums, query_grad):
        dk, dv = sums
        norm, q = block["norm"], block["q"]
        along = jnp.sum(q * dk, axis=0, keepdims=True) * (norm * norm)
        dk = norm * (dk - along * q)
        if query_grad is not None:
            dk = dk + query_grad
        return [dk.astype(BF16), dv.astype(BF16)]

    none = jnp.zeros((h, n), BF16)
    turned = [
        jnp.concatenate(pieces, axis=0)
        for pieces in (
            result(block_z, sums_z, None),
            [*result(block_a, sums_a, dq_a), out_a, none],
            [*result(block_b, sums_b, dq_b), none, out_b],
        )
    ]
    sends = []
    for t, used in enumerate((first, slice(0, n), slice(0, n), last)):
        places = slice(t * group // 4, (t + 1) * group // 4)
        peers = slice(t * PEERS // 4, (t + 1) * PEERS // 4)
        s_z, s_a, s_b = (
            nt(give_ref[i, places, used], x[:, used]).reshape(PEERS // 4, 8, x.shape[0])
            for i, x in enumerate(turned)
        )
        mixed = s_a[:, :, 128:] + s_b[:, :, 128:]
        out_ref[peers] = rows_of([s_z, s_a[:, :, :128], s_b[:, :, :128]], mixed)
        sends.append(
            pltpu.make_async_copy(out_ref.at[peers], out_hbm.at[peers], sems.at[t])
        )
        sends[-1].start()
    for copy in sends:
        copy.wait()


def restore_kernel(ret_ref, code_ref, att_ref, dqk_ref, dv_ref):
    code = column(code_ref[...]).astype(I32)
    block, rank = code >> 3, code & 7
    chip, odd = block >> 1, (block & 1) == 1
    group = 8 * CHIPS
    own_at = chip * 8 + rank
    prior_at = jnp.where(odd, ((chip + 1) & (CHIPS - 1)) * 8 + rank, -1)
    chosen = jnp.concatenate(
        [
            lanes_equal(prior_at, group),
            lanes_equal(jnp.where(odd, -1, own_at), group),
            lanes_equal(jnp.where(odd, own_at, -1), group),
        ],
        axis=1,
    )
    tiles = [tiles_of(ret_ref[:, c].astype(F32)) for c in range(2)]
    values = [jnp.concatenate([t[i] for t in tiles], axis=1) for i in range(4)]
    grads = mm(chosen, jnp.concatenate(values[:3], axis=0)).astype(BF16)
    outs = mm(lanes_equal(own_at, group), values[3])
    h = HEAD_DIM
    odd_h = odd[:, :h]
    att_ref[...] = jnp.concatenate(
        [
            jnp.where(odd_h, outs[:, h : 2 * h], outs[:, :h]),
            jnp.where(odd_h, outs[:, 3 * h :], outs[:, 2 * h : 3 * h]),
        ],
        axis=1,
    ).astype(BF16)
    dqk_ref[...] = jnp.concatenate([grads[:, :h], grads[:, 2 * h : 3 * h]], axis=1)
    dv_ref[...] = jnp.concatenate([grads[:, h : 2 * h], grads[:, 3 * h :]], axis=1)


hbm = pl.BlockSpec(memory_space=pltpu.HBM)
vmem = pl.BlockSpec(memory_space=pltpu.VMEM)


def struct(shape, dtype):
    return jax.ShapeDtypeStruct(shape, dtype)


def params(mib):
    return pltpu.CompilerParams(vmem_limit_bytes=mib * 1024 * 1024)


def in_hbm(x):
    return pltpu.with_memory_space_constraint(x, pltpu.HBM)


hbm = pl.BlockSpec(memory_space=pltpu.HBM)
vmem = pl.BlockSpec(memory_space=pltpu.VMEM)


def pack(slots, q, v, g):
    n = q.shape[0]
    return pl.pallas_call(
        pack_kernel,
        in_specs=[pl.BlockSpec(memory_space=pltpu.HBM)] * 4,
        out_shape=(struct((CHIPS, 2, ROWS, 128), BF16), struct((1, n), I32)),
        scratch_shapes=[pltpu.VMEM((1, n), I32)]
        + [pltpu.VMEM((n, 128), BF16)] * 3
        + [pltpu.SemaphoreType.DMA((4,))],
        compiler_params=params(24),
        name="pack",
    )(*map(in_hbm, (slots, q, v, g)))


def meta(orders, code):
    return pl.pallas_call(
        meta_kernel,
        out_shape=struct((8, BLOCK), I32),
        compiler_params=params(24),
        cost_estimate=pl.CostEstimate(
            flops=META_FLOPS, bytes_accessed=32768, transcendentals=0
        ),
        name="meta",
    )(orders, code)


def attend(arrived, table):
    shape = (PEERS, ROWS, 128)
    return pl.pallas_call(
        attend_kernel,
        in_specs=[vmem, vmem],
        out_specs=hbm,
        out_shape=struct(shape, BF16),
        scratch_shapes=[
            pltpu.VMEM((3, 8 * PEERS, BLOCK), BF16),
            pltpu.VMEM(shape, BF16),
            pltpu.SemaphoreType.DMA((4,)),
        ],
        compiler_params=params(40),
        name="attend",
    )(arrived, table)


def restore(returned, code):
    n = code.shape[1]
    return pl.pallas_call(
        restore_kernel,
        out_shape=[struct((n, 128), BF16)] * 3,
        compiler_params=params(24),
        name="restore",
    )(returned, code)


def exchange(message):
    return lax.all_to_all(message, "seq", split_axis=0, concat_axis=0, tiled=True)


def per_device(shared_qk, value_rows, out_grad, bucket_order, inverse_order):
    peers = range(PEERS)
    before = lax.ppermute(bucket_order, "seq", [(i, (i + 2) % PEERS) for i in peers])
    held = jnp.concatenate([bucket_order, before], axis=0)
    other = lax.ppermute(held, "seq", [(i, i ^ 1) for i in peers])
    even = lax.axis_index("seq") & 1 == 0
    near = jnp.concatenate(
        [
            jnp.where(even, other[1:], before),
            jnp.where(even, bucket_order, other[:1]),
            jnp.where(even, other[:1], bucket_order),
        ],
        axis=0,
    )
    message, code = pack(inverse_order, shared_qk, value_rows, out_grad)
    arrived = exchange(message.reshape(PEERS, ROWS, 128))
    returned = exchange(attend(arrived, meta(near, code)))
    return tuple(restore(returned.reshape(CHIPS, 2, ROWS, 128), code))


def solution(mesh):
    rows, orders = P("seq", "head"), P("head", "seq")
    return jax.shard_map(
        per_device,
        mesh=mesh,
        in_specs=(rows, rows, rows, orders, orders),
        out_specs=(rows, rows, rows),
        check_vma=False,
    )
```

```python
import jax
import jax.numpy as jnp
from jax import lax
from jax.experimental import pallas as pl
from jax.experimental.pallas import tpu as pltpu
from jax.sharding import PartitionSpec as P

HEAD_DIM = 64
BLOCK = 512
RANKS = 6
PEERS = 128
CHIPS = 64
ROWS = 24

META_FLOPS = 12 * 10**9

log2_e = 1.4426950408889634
self_score = -100000.0 * log2_e
masked_score = -1000000000.0 * log2_e
norm_eps = 1e-06

F32 = jnp.float32
BF16 = jnp.bfloat16
I32 = jnp.int32


def iota(shape, dim):
    return lax.broadcasted_iota(I32, shape, dim)


def mm(a, b):
    return jnp.dot(a, b, preferred_element_type=F32)


def ones_where(mask):
    return jnp.where(mask, F32(1), F32(0)).astype(BF16)


def column(row):
    return jnp.transpose(jnp.broadcast_to(row.astype(F32), (128, row.shape[1])))


def lanes_equal(index_col, width):
    lane = iota(index_col.shape, 1)
    return jnp.concatenate(
        [ones_where(index_col == lane + 128 * n) for n in range(width // 128)], axis=1
    )


def rows_equal(index_row, height):
    return ones_where(iota((height, index_row.shape[1]), 0) == index_row)


def tiles_of(rows):
    count = rows.shape[0] * 8
    mixed = jnp.concatenate(
        [rows[:, 6:8], rows[:, 14:16], rows[:, 22:24], jnp.zeros_like(rows[:, :2])], axis=1
    )
    tiles = [rows[:, 8 * i : 8 * i + 8] for i in range(3)] + [mixed]
    return [t.reshape(count, 128).astype(BF16) for t in tiles]


def rows_of(tiles, mixed):
    pieces = []
    for i, tile in enumerate(tiles):
        pieces += [tile[:, :6], mixed[:, 2 * i : 2 * i + 2]]
    return jnp.concatenate(pieces, axis=1).astype(BF16)


def pack_kernel(slot_hbm, q_hbm, v_hbm, g_hbm, msg_ref, code_ref, slot_ref, q_ref, v_ref, g_ref, sems):
    copies = [
        pltpu.make_async_copy(src, dst, sems.at[i])
        for i, (src, dst) in enumerate(
            [(slot_hbm, slot_ref), (q_hbm, q_ref), (v_hbm, v_ref), (g_hbm, g_ref)]
        )
    ]
    for copy in copies:
        copy.start()
    copies[0].wait()
    block = slot_ref[...] >> 9
    local = block.shape[1]
    member = iota((PEERS, local), 0) == block
    before = ones_where(iota((local, local), 0) < iota((local, local), 1))
    counts = mm(ones_where(member), before)
    rank = jnp.sum(jnp.where(member, counts, F32(0)), axis=0, keepdims=True)
    code = block * 8 + rank.astype(I32)
    code_ref[...] = code

    def choose(offset):
        shape = (CHIPS, 8, 128)
        want = 16 * iota(shape, 0) + iota(shape, 1) + offset
        want = jnp.where(want < 0, want + 8 * PEERS, want).reshape(CHIPS * 8, 128)
        return jnp.concatenate(
            [ones_where(want == code[:, 128 * n : 128 * n + 128]) for n in range(local // 128)],
            axis=1,
        )

    chosen = [choose(offset) for offset in (-8, 0, 8)]
    for copy in copies[1:]:
        copy.wait()
    q, v, g = q_ref[...], v_ref[...], g_ref[...]
    h0, h1 = slice(0, HEAD_DIM), slice(HEAD_DIM, 2 * HEAD_DIM)
    none = jnp.zeros((local, HEAD_DIM), BF16)
    qv = jnp.concatenate([q[:, h0], v[:, h0], q[:, h1], v[:, h1]], axis=1)
    ga = jnp.concatenate([g[:, h0], none, g[:, h1], none], axis=1)
    gb = jnp.concatenate([none, g[:, h0], none, g[:, h1]], axis=1)
    tiles = [mm(one, qv) for one in chosen]
    mixed = mm(jnp.concatenate(chosen[1:], axis=1), jnp.concatenate([ga, gb], axis=0))
    for c in range(2):
        cols = slice(128 * c, 128 * c + 128)
        msg_ref[:, c] = rows_of(
            [t[:, cols].reshape(CHIPS, 8, 128) for t in tiles],
            mixed[:, cols].reshape(CHIPS, 8, 128),
        )


def meta_kernel(orders_ref, code_ref, table_ref):
    n = BLOCK
    lane = iota((n, n), 1)
    at = iota((1, n), 1)

    def wide(col):
        return jnp.concatenate([col] * (n // 128), axis=1)

    for i in range(3):
        pos = orders_ref[i : i + 1].astype(F32)
        pos_col = wide(column(pos))
        place = jnp.sum(jnp.where(pos_col < pos, F32(1), F32(0)), axis=0, keepdims=True)
        place_col = wide(column(place)).astype(I32)
        ordered = jnp.sum(jnp.where(place_col == lane, pos_col, F32(0)), axis=0, keepdims=True)
        source = ordered.astype(I32) >> 9
        start = (source << 9).astype(F32)
        offset = jnp.sum(
            jnp.where(wide(column(ordered)) < start, F32(1), F32(0)), axis=0, keepdims=True
        )
        table_ref[i : i + 1] = ordered.astype(I32)
        table_ref[i + 3 : i + 4] = source * 8 + at - offset.astype(I32)
    table_ref[6:7] = code_ref[...]
    table_ref[7:8] = jnp.zeros((1, n), I32)


def nt(a, b):
    return lax.dot_general(a, b, (((1,), (1,)), ((), ())), preferred_element_type=F32)


def tn(a, b):
    return lax.dot_general(a, b, (((0,), (0,)), ((), ())), preferred_element_type=F32)


def two_terms(x):
    high = x.astype(BF16)
    return high, (x - high.astype(F32)).astype(BF16)


def attend_kernel(arr_ref, rows_ref, out_ref, give_ref):
    n, half, group = BLOCK, BLOCK // 2, 8 * PEERS
    part_z, part_a, part_b, part_g = tiles_of(arr_ref[...].astype(F32))
    reach = 3 * group // 4

    def take(i, part):
        code = rows_ref[3 + i : 4 + i]
        first, last = slice(0, half), slice(half, n)
        give_ref[i, :reach, first] = rows_equal(code[:, first], reach)
        give_ref[i, group - reach :, last] = rows_equal(code[:, last] - (group - reach), reach)
        return jnp.concatenate(
            [
                tn(part[:reach], give_ref[i, :reach, first]),
                tn(part[group - reach :], give_ref[i, group - reach :, last]),
            ],
            axis=1,
        )

    give_ref[:, reach:, :half] = jnp.zeros((3, group - reach, half), BF16)
    give_ref[:, : group - reach, half:] = jnp.zeros((3, group - reach, half), BF16)
    x_z = take(0, part_z)
    x_a = take(1, jnp.concatenate([part_a, part_g], axis=1))
    x_b = take(2, jnp.concatenate([part_b, part_g], axis=1))
    h = HEAD_DIM
    g_a, g_b = x_a[2 * h : 3 * h], x_b[3 * h :]
    pad = jnp.zeros((14, n), BF16)
    ones = jnp.ones((16, n), BF16)

    def block_of(x):
        q, v = x[:h], x[h : 2 * h]
        norm = lax.rsqrt(jnp.sum(q * q, axis=0, keepdims=True) + norm_eps)
        return dict(
            q=q,
            qb=q.astype(BF16),
            vb=jnp.concatenate([v.astype(BF16), ones], axis=0),
            norm=norm,
            scale=norm * log2_e,
            key=(q * norm).astype(BF16),
        )

    block_z, block_a, block_b = [block_of(x) for x in (x_z, x_a, x_b)]

    first, last = slice(0, half), slice(half, n)
    row, col = iota((half, half), 0), iota((half, half), 1)

    def low_high(x):
        return x[:half], x[half:]

    def late(x, y):
        return jnp.concatenate([x[:, first], x[:, last] + y], axis=1)

    def item(prior, own, grads, prior_pos, own_pos):
        q = own["qb"]
        pos = jnp.concatenate([column(own_pos)] * (n // 128), axis=1)
        s0 = tn(q, prior["qb"]) * prior["scale"]
        s0 = jnp.where(prior_pos.astype(F32) < pos, s0, masked_score)
        s1 = tn(q, own["qb"][:, first]) * own["scale"][:, first]
        s2 = tn(q[:, last], own["qb"][:, last]) * own["scale"][:, last]

        def triangle(s):
            return jnp.where(col < row, s, jnp.where(col == row, self_score, masked_score))

        s1 = jnp.concatenate([triangle(s1[:half]), s1[half:]], axis=0)
        s2 = triangle(s2)
        top0, top1, top2 = (jnp.max(s, axis=1, keepdims=True) for s in (s0, s1, s2))
        top_low, top_high = low_high(jnp.maximum(top0, top1))
        top_high = jnp.maximum(top_high, top2)
        top = jnp.concatenate([top_low, top_high], axis=0)
        p0, p1, p2 = jnp.exp2(s0 - top), jnp.exp2(s1 - top), jnp.exp2(s2 - top_high)
        b0, b1, b2 = p0.astype(BF16), p1.astype(BF16), p2.astype(BF16)
        v0, v1, v2 = prior["vb"], own["vb"][:, first], own["vb"][:, last]
        summed = late(nt(v0, b0) + nt(v1, b1), nt(v2, b2))
        inverse = 1.0 / summed[h : h + 1]
        out = (summed[:h] * inverse).astype(BF16)
        grad = (grads * inverse).astype(BF16)
        delta = jnp.sum(grad.astype(F32) * out.astype(F32), axis=0, keepdims=True)
        left = jnp.concatenate([grad, *two_terms(-delta), pad], axis=0)
        d0 = (p0 * tn(left, v0)).astype(BF16)
        d1 = (p1 * tn(left, v1)).astype(BF16)
        d2 = (p2 * tn(left[:, last], v2)).astype(BF16)
        dq = late(
            nt(prior["key"], d0) + nt(own["key"][:, first], d1), nt(own["key"][:, last], d2)
        )
        sums_prior = (mm(q, d0), mm(grad, b0))
        sums_own = tuple(
            jnp.concatenate([mm(x, lo), mm(x[:, last], hi)], axis=1)
            for x, lo, hi in ((q, d1, d2), (grad, b1, b2))
        )
        return out, dq, sums_prior, sums_own

    pos_z, pos_a, pos_b = rows_ref[0:1], rows_ref[1:2], rows_ref[2:3]
    out_a, dq_a, sums_z, sums_a = item(block_z, block_a, g_a, pos_z, pos_a)
    out_b, dq_b, more_a, sums_b = item(block_a, block_b, g_b, pos_a, pos_b)
    sums_a = (sums_a[0] + more_a[0], sums_a[1] + more_a[1])

    def result(block, sums, query_grad):
        dk, dv = sums
        norm, q = block["norm"], block["q"]
        along = jnp.sum(q * dk, axis=0, keepdims=True) * (norm * norm)
        dk = norm * (dk - along * q)
        if query_grad is not None:
            dk = dk + query_grad
        return [dk.astype(BF16), dv.astype(BF16)]

    none = jnp.zeros((h, n), BF16)
    turned = [
        jnp.concatenate(pieces, axis=0)
        for pieces in (
            result(block_z, sums_z, None),
            [*result(block_a, sums_a, dq_a), out_a, none],
            [*result(block_b, sums_b, dq_b), none, out_b],
        )
    ]
    for t, used in enumerate((first, slice(0, n), slice(0, n), last)):
        places = slice(t * group // 4, (t + 1) * group // 4)
        peers = slice(t * PEERS // 4, (t + 1) * PEERS // 4)
        s_z, s_a, s_b = (
            nt(give_ref[i, places, used], x[:, used]).reshape(PEERS // 4, 8, x.shape[0])
            for i, x in enumerate(turned)
        )
        mixed = s_a[:, :, 128:] + s_b[:, :, 128:]
        out_ref[peers] = rows_of([s_z, s_a[:, :, :128], s_b[:, :, :128]], mixed)


def restore_kernel(ret_ref, code_ref, att_ref, dqk_ref, dv_ref):
    code = column(code_ref[...]).astype(I32)
    block, rank = code >> 3, code & 7
    chip, odd = block >> 1, (block & 1) == 1
    group = 8 * CHIPS
    own_at = chip * 8 + rank
    prior_at = jnp.where(odd, ((chip + 1) & (CHIPS - 1)) * 8 + rank, -1)
    chosen = jnp.concatenate(
        [
            lanes_equal(prior_at, group),
            lanes_equal(jnp.where(odd, -1, own_at), group),
            lanes_equal(jnp.where(odd, own_at, -1), group),
        ],
        axis=1,
    )
    tiles = [tiles_of(ret_ref[:, c].astype(F32)) for c in range(2)]
    values = [jnp.concatenate([t[i] for t in tiles], axis=1) for i in range(4)]
    grads = mm(chosen, jnp.concatenate(values[:3], axis=0)).astype(BF16)
    outs = mm(lanes_equal(own_at, group), values[3])
    h = HEAD_DIM
    odd_h = odd[:, :h]
    att_ref[...] = jnp.concatenate(
        [
            jnp.where(odd_h, outs[:, h : 2 * h], outs[:, :h]),
            jnp.where(odd_h, outs[:, 3 * h :], outs[:, 2 * h : 3 * h]),
        ],
        axis=1,
    ).astype(BF16)
    dqk_ref[...] = jnp.concatenate([grads[:, :h], grads[:, 2 * h : 3 * h]], axis=1)
    dv_ref[...] = jnp.concatenate([grads[:, h : 2 * h], grads[:, 3 * h :]], axis=1)


def struct(shape, dtype):
    return jax.ShapeDtypeStruct(shape, dtype)


def params(mib):
    return pltpu.CompilerParams(vmem_limit_bytes=mib * 1024 * 1024)


def in_hbm(x):
    return pltpu.with_memory_space_constraint(x, pltpu.HBM)


def pack(slots, q, v, g):
    n = q.shape[0]
    return pl.pallas_call(
        pack_kernel,
        in_specs=[pl.BlockSpec(memory_space=pltpu.HBM)] * 4,
        out_shape=(struct((CHIPS, 2, ROWS, 128), BF16), struct((1, n), I32)),
        scratch_shapes=[pltpu.VMEM((1, n), I32)]
        + [pltpu.VMEM((n, 128), BF16)] * 3
        + [pltpu.SemaphoreType.DMA((4,))],
        compiler_params=params(24),
        name="pack",
    )(*map(in_hbm, (slots, q, v, g)))


def meta(orders, code):
    return pl.pallas_call(
        meta_kernel,
        out_shape=struct((8, BLOCK), I32),
        compiler_params=params(24),
        cost_estimate=pl.CostEstimate(
            flops=META_FLOPS, bytes_accessed=32768, transcendentals=0
        ),
        name="meta",
    )(orders, code)


def attend(arrived, table):
    shape = (PEERS, ROWS, 128)
    return pl.pallas_call(
        attend_kernel,
        out_shape=struct(shape, BF16),
        scratch_shapes=[
            pltpu.VMEM((3, 8 * PEERS, BLOCK), BF16),
        ],
        compiler_params=params(40),
        name="attend",
    )(arrived, table)


def restore(returned, code):
    n = code.shape[1]
    return pl.pallas_call(
        restore_kernel,
        out_shape=[struct((n, 128), BF16)] * 3,
        compiler_params=params(24),
        name="restore",
    )(returned, code)


def exchange(message):
    return lax.all_to_all(message, "seq", split_axis=0, concat_axis=0, tiled=True)


def per_device(shared_qk, value_rows, out_grad, bucket_order, inverse_order):
    peers = range(PEERS)
    before = lax.ppermute(bucket_order, "seq", [(i, (i + 2) % PEERS) for i in peers])
    held = jnp.concatenate([bucket_order, before], axis=0)
    other = lax.ppermute(held, "seq", [(i, i ^ 1) for i in peers])
    even = lax.axis_index("seq") & 1 == 0
    near = jnp.concatenate(
        [
            jnp.where(even, other[1:], before),
            jnp.where(even, bucket_order, other[:1]),
            jnp.where(even, other[:1], bucket_order),
        ],
        axis=0,
    )
    message, code = pack(inverse_order, shared_qk, value_rows, out_grad)
    arrived = exchange(message.reshape(PEERS, ROWS, 128))
    returned = exchange(attend(arrived, meta(near, code)))
    return tuple(restore(returned.reshape(CHIPS, 2, ROWS, 128), code))


def solution(mesh):
    rows, orders = P("seq", "head"), P("head", "seq")
    return jax.shard_map(
        per_device,
        mesh=mesh,
        in_specs=(rows, rows, rows, orders, orders),
        out_specs=(rows, rows, rows),
        check_vma=False,
    )
```

```python
import jax
import jax.numpy as jnp
from jax import lax
from jax.experimental import pallas as pl
from jax.experimental.pallas import tpu as pltpu
from jax.sharding import PartitionSpec as P

HEAD_DIM = 64
BLOCK = 512
RANKS = 6
PEERS = 128
CHIPS = 64
ROWS = 24

META_FLOPS = 12 * 10**9

log2_e = 1.4426950408889634
self_score = -100000.0 * log2_e
masked_score = -1000000000.0 * log2_e
norm_eps = 1e-06

F32 = jnp.float32
BF16 = jnp.bfloat16
I32 = jnp.int32


def iota(shape, dim):
    return lax.broadcasted_iota(I32, shape, dim)


def mm(a, b):
    return jnp.dot(a, b, preferred_element_type=F32)


def ones_where(mask):
    return jnp.where(mask, F32(1), F32(0)).astype(BF16)


def column(row):
    return jnp.transpose(jnp.broadcast_to(row.astype(F32), (128, row.shape[1])))


def lanes_equal(index_col, width):
    lane = iota(index_col.shape, 1)
    return jnp.concatenate(
        [ones_where(index_col == lane + 128 * n) for n in range(width // 128)], axis=1
    )


def rows_equal(index_row, height):
    return ones_where(iota((height, index_row.shape[1]), 0) == index_row)


def tiles_of(rows):
    count = rows.shape[0] * 8
    mixed = jnp.concatenate(
        [rows[:, 6:8], rows[:, 14:16], rows[:, 22:24], jnp.zeros_like(rows[:, :2])], axis=1
    )
    tiles = [rows[:, 8 * i : 8 * i + 8] for i in range(3)] + [mixed]
    return [t.reshape(count, 128).astype(BF16) for t in tiles]


def rows_of(tiles, mixed):
    pieces = []
    for i, tile in enumerate(tiles):
        pieces += [tile[:, :6], mixed[:, 2 * i : 2 * i + 2]]
    return jnp.concatenate(pieces, axis=1).astype(BF16)


def pack_kernel(slot_hbm, q_hbm, v_hbm, g_hbm, msg_ref, code_ref, slot_ref, q_ref, v_ref, g_ref, sems):
    copies = [
        pltpu.make_async_copy(src, dst, sems.at[i])
        for i, (src, dst) in enumerate(
            [(slot_hbm, slot_ref), (q_hbm, q_ref), (v_hbm, v_ref), (g_hbm, g_ref)]
        )
    ]
    for copy in copies:
        copy.start()
    copies[0].wait()
    block = slot_ref[...] >> 9
    local = block.shape[1]
    member = iota((PEERS, local), 0) == block
    before = ones_where(iota((local, local), 0) < iota((local, local), 1))
    counts = mm(ones_where(member), before)
    rank = jnp.sum(jnp.where(member, counts, F32(0)), axis=0, keepdims=True)
    code = block * 8 + rank.astype(I32)
    code_ref[...] = code

    def choose(offset):
        shape = (CHIPS, 8, 128)
        want = 16 * iota(shape, 0) + iota(shape, 1) + offset
        want = jnp.where(want < 0, want + 8 * PEERS, want).reshape(CHIPS * 8, 128)
        return jnp.concatenate(
            [ones_where(want == code[:, 128 * n : 128 * n + 128]) for n in range(local // 128)],
            axis=1,
        )

    chosen = [choose(offset) for offset in (-8, 0, 8)]
    for copy in copies[1:]:
        copy.wait()
    q, v, g = q_ref[...], v_ref[...], g_ref[...]
    h0, h1 = slice(0, HEAD_DIM), slice(HEAD_DIM, 2 * HEAD_DIM)
    none = jnp.zeros((local, HEAD_DIM), BF16)
    qv = jnp.concatenate([q[:, h0], v[:, h0], q[:, h1], v[:, h1]], axis=1)
    ga = jnp.concatenate([g[:, h0], none, g[:, h1], none], axis=1)
    gb = jnp.concatenate([none, g[:, h0], none, g[:, h1]], axis=1)
    tiles = [mm(one, qv) for one in chosen]
    mixed = mm(jnp.concatenate(chosen[1:], axis=1), jnp.concatenate([ga, gb], axis=0))
    for c in range(2):
        cols = slice(128 * c, 128 * c + 128)
        msg_ref[:, c] = rows_of(
            [t[:, cols].reshape(CHIPS, 8, 128) for t in tiles],
            mixed[:, cols].reshape(CHIPS, 8, 128),
        )


def meta_kernel(orders_ref, code_ref, table_ref):
    n = BLOCK
    lane = iota((n, n), 1)
    at = iota((1, n), 1)

    def wide(col):
        return jnp.concatenate([col] * (n // 128), axis=1)

    for i in range(3):
        pos = orders_ref[i : i + 1].astype(F32)
        pos_col = wide(column(pos))
        place = jnp.sum(jnp.where(pos_col < pos, F32(1), F32(0)), axis=0, keepdims=True)
        place_col = wide(column(place)).astype(I32)
        ordered = jnp.sum(jnp.where(place_col == lane, pos_col, F32(0)), axis=0, keepdims=True)
        source = ordered.astype(I32) >> 9
        start = (source << 9).astype(F32)
        offset = jnp.sum(
            jnp.where(wide(column(ordered)) < start, F32(1), F32(0)), axis=0, keepdims=True
        )
        table_ref[i : i + 1] = ordered.astype(I32)
        table_ref[i + 3 : i + 4] = source * 8 + at - offset.astype(I32)
    table_ref[6:7] = code_ref[...]
    table_ref[7:8] = jnp.zeros((1, n), I32)


def nt(a, b):
    return lax.dot_general(a, b, (((1,), (1,)), ((), ())), preferred_element_type=F32)


def tn(a, b):
    return lax.dot_general(a, b, (((0,), (0,)), ((), ())), preferred_element_type=F32)


def two_terms(x):
    high = x.astype(BF16)
    return high, (x - high.astype(F32)).astype(BF16)


def attend_kernel(arr_ref, rows_ref, out_ref, give_ref):
    n, half, group = BLOCK, BLOCK // 2, 8 * PEERS
    part_z, part_a, part_b, part_g = tiles_of(arr_ref[...].astype(F32))
    reach = 3 * group // 4

    def take(i, part):
        code = rows_ref[3 + i : 4 + i]
        first, last = slice(0, half), slice(half, n)
        give_ref[i, :reach, first] = rows_equal(code[:, first], reach)
        give_ref[i, group - reach :, last] = rows_equal(code[:, last] - (group - reach), reach)
        return jnp.concatenate(
            [
                tn(part[:reach], give_ref[i, :reach, first]),
                tn(part[group - reach :], give_ref[i, group - reach :, last]),
            ],
            axis=1,
        )

    give_ref[:, reach:, :half] = jnp.zeros((3, group - reach, half), BF16)
    give_ref[:, : group - reach, half:] = jnp.zeros((3, group - reach, half), BF16)
    x_z = take(0, part_z)
    x_a = take(1, jnp.concatenate([part_a, part_g], axis=1))
    x_b = take(2, jnp.concatenate([part_b, part_g], axis=1))
    h = HEAD_DIM
    g_a, g_b = x_a[2 * h : 3 * h], x_b[3 * h :]
    pad = jnp.zeros((14, n), BF16)
    ones = jnp.ones((16, n), BF16)

    def block_of(x):
        q, v = x[:h], x[h : 2 * h]
        norm = lax.rsqrt(jnp.sum(q * q, axis=0, keepdims=True) + norm_eps)
        return dict(
            q=q,
            qb=q.astype(BF16),
            vb=jnp.concatenate([v.astype(BF16), ones], axis=0),
            norm=norm,
            scale=norm * log2_e,
            key=(q * norm).astype(BF16),
        )

    block_z, block_a, block_b = [block_of(x) for x in (x_z, x_a, x_b)]

    first, last = slice(0, half), slice(half, n)
    row, col = iota((half, half), 0), iota((half, half), 1)

    def low_high(x):
        return x[:half], x[half:]

    def late(x, y):
        return jnp.concatenate([x[:, first], x[:, last] + y], axis=1)

    def item(prior, own, grads, prior_pos, own_pos):
        q = own["qb"]
        pos = jnp.concatenate([column(own_pos)] * (n // 128), axis=1)
        s0 = tn(q, prior["qb"]) * prior["scale"]
        s0 = jnp.where(prior_pos.astype(F32) < pos, s0, masked_score)
        s1 = tn(q, own["qb"][:, first]) * own["scale"][:, first]
        s2 = tn(q[:, last], own["qb"][:, last]) * own["scale"][:, last]
        yield

        def triangle(s):
            return jnp.where(col < row, s, jnp.where(col == row, self_score, masked_score))

        s1 = jnp.concatenate([triangle(s1[:half]), s1[half:]], axis=0)
        s2 = triangle(s2)
        top0, top1, top2 = (jnp.max(s, axis=1, keepdims=True) for s in (s0, s1, s2))
        top_low, top_high = low_high(jnp.maximum(top0, top1))
        top_high = jnp.maximum(top_high, top2)
        top = jnp.concatenate([top_low, top_high], axis=0)
        p0, p1, p2 = jnp.exp2(s0 - top), jnp.exp2(s1 - top), jnp.exp2(s2 - top_high)
        b0, b1, b2 = p0.astype(BF16), p1.astype(BF16), p2.astype(BF16)
        yield
        v0, v1, v2 = prior["vb"], own["vb"][:, first], own["vb"][:, last]
        summed = late(nt(v0, b0) + nt(v1, b1), nt(v2, b2))
        inverse = 1.0 / summed[h : h + 1]
        out = (summed[:h] * inverse).astype(BF16)
        grad = (grads * inverse).astype(BF16)
        delta = jnp.sum(grad.astype(F32) * out.astype(F32), axis=0, keepdims=True)
        left = jnp.concatenate([grad, *two_terms(-delta), pad], axis=0)
        yield
        d0 = (p0 * tn(left, v0)).astype(BF16)
        d1 = (p1 * tn(left, v1)).astype(BF16)
        d2 = (p2 * tn(left[:, last], v2)).astype(BF16)
        yield
        dq = late(
            nt(prior["key"], d0) + nt(own["key"][:, first], d1), nt(own["key"][:, last], d2)
        )
        sums_prior = (mm(q, d0), mm(grad, b0))
        sums_own = tuple(
            jnp.concatenate([mm(x, lo), mm(x[:, last], hi)], axis=1)
            for x, lo, hi in ((q, d1, d2), (grad, b1, b2))
        )
        yield out, dq, sums_prior, sums_own

    pos_z, pos_a, pos_b = rows_ref[0:1], rows_ref[1:2], rows_ref[2:3]
    items = [
        item(block_z, block_a, g_a, pos_z, pos_a),
        item(block_a, block_b, g_b, pos_a, pos_b),
    ]
    ends = {}
    for i in (0, 0, 1, 0, 1, 0, 1, 0, 1, 1):
        ends[i] = next(items[i])
    out_a, dq_a, sums_z, sums_a = ends[0]
    out_b, dq_b, more_a, sums_b = ends[1]
    sums_a = (sums_a[0] + more_a[0], sums_a[1] + more_a[1])

    def result(block, sums, query_grad):
        dk, dv = sums
        norm, q = block["norm"], block["q"]
        along = jnp.sum(q * dk, axis=0, keepdims=True) * (norm * norm)
        dk = norm * (dk - along * q)
        if query_grad is not None:
            dk = dk + query_grad
        return [dk.astype(BF16), dv.astype(BF16)]

    none = jnp.zeros((h, n), BF16)
    turned = [
        jnp.concatenate(pieces, axis=0)
        for pieces in (
            result(block_z, sums_z, None),
            [*result(block_a, sums_a, dq_a), out_a, none],
            [*result(block_b, sums_b, dq_b), none, out_b],
        )
    ]
    for t, used in enumerate((first, slice(0, n), slice(0, n), last)):
        places = slice(t * group // 4, (t + 1) * group // 4)
        peers = slice(t * PEERS // 4, (t + 1) * PEERS // 4)
        s_z, s_a, s_b = (
            nt(give_ref[i, places, used], x[:, used]).reshape(PEERS // 4, 8, x.shape[0])
            for i, x in enumerate(turned)
        )
        mixed = s_a[:, :, 128:] + s_b[:, :, 128:]
        out_ref[peers] = rows_of([s_z, s_a[:, :, :128], s_b[:, :, :128]], mixed)


def restore_kernel(ret_ref, code_ref, att_ref, dqk_ref, dv_ref):
    code = column(code_ref[...]).astype(I32)
    block, rank = code >> 3, code & 7
    chip, odd = block >> 1, (block & 1) == 1
    group = 8 * CHIPS
    own_at = chip * 8 + rank
    prior_at = jnp.where(odd, ((chip + 1) & (CHIPS - 1)) * 8 + rank, -1)
    chosen = jnp.concatenate(
        [
            lanes_equal(prior_at, group),
            lanes_equal(jnp.where(odd, -1, own_at), group),
            lanes_equal(jnp.where(odd, own_at, -1), group),
        ],
        axis=1,
    )
    tiles = [tiles_of(ret_ref[:, c].astype(F32)) for c in range(2)]
    values = [jnp.concatenate([t[i] for t in tiles], axis=1) for i in range(4)]
    grads = mm(chosen, jnp.concatenate(values[:3], axis=0)).astype(BF16)
    outs = mm(lanes_equal(own_at, group), values[3])
    h = HEAD_DIM
    odd_h = odd[:, :h]
    att_ref[...] = jnp.concatenate(
        [
            jnp.where(odd_h, outs[:, h : 2 * h], outs[:, :h]),
            jnp.where(odd_h, outs[:, 3 * h :], outs[:, 2 * h : 3 * h]),
        ],
        axis=1,
    ).astype(BF16)
    dqk_ref[...] = jnp.concatenate([grads[:, :h], grads[:, 2 * h : 3 * h]], axis=1)
    dv_ref[...] = jnp.concatenate([grads[:, h : 2 * h], grads[:, 3 * h :]], axis=1)


def struct(shape, dtype):
    return jax.ShapeDtypeStruct(shape, dtype)


def params(mib):
    return pltpu.CompilerParams(vmem_limit_bytes=mib * 1024 * 1024)


def in_hbm(x):
    return pltpu.with_memory_space_constraint(x, pltpu.HBM)


def pack(slots, q, v, g):
    n = q.shape[0]
    return pl.pallas_call(
        pack_kernel,
        in_specs=[pl.BlockSpec(memory_space=pltpu.HBM)] * 4,
        out_shape=(struct((CHIPS, 2, ROWS, 128), BF16), struct((1, n), I32)),
        scratch_shapes=[pltpu.VMEM((1, n), I32)]
        + [pltpu.VMEM((n, 128), BF16)] * 3
        + [pltpu.SemaphoreType.DMA((4,))],
        compiler_params=params(24),
        name="pack",
    )(*map(in_hbm, (slots, q, v, g)))


def meta(orders, code):
    return pl.pallas_call(
        meta_kernel,
        out_shape=struct((8, BLOCK), I32),
        compiler_params=params(24),
        cost_estimate=pl.CostEstimate(
            flops=META_FLOPS, bytes_accessed=32768, transcendentals=0
        ),
        name="meta",
    )(orders, code)


def attend(arrived, table):
    shape = (PEERS, ROWS, 128)
    return pl.pallas_call(
        attend_kernel,
        out_shape=struct(shape, BF16),
        scratch_shapes=[
            pltpu.VMEM((3, 8 * PEERS, BLOCK), BF16),
        ],
        compiler_params=params(40),
        name="attend",
    )(arrived, table)


def restore(returned, code):
    n = code.shape[1]
    return pl.pallas_call(
        restore_kernel,
        out_shape=[struct((n, 128), BF16)] * 3,
        compiler_params=params(24),
        name="restore",
    )(returned, code)


def exchange(message):
    return lax.all_to_all(message, "seq", split_axis=0, concat_axis=0, tiled=True)


def per_device(shared_qk, value_rows, out_grad, bucket_order, inverse_order):
    peers = range(PEERS)
    before = lax.ppermute(bucket_order, "seq", [(i, (i + 2) % PEERS) for i in peers])
    held = jnp.concatenate([bucket_order, before], axis=0)
    other = lax.ppermute(held, "seq", [(i, i ^ 1) for i in peers])
    even = lax.axis_index("seq") & 1 == 0
    near = jnp.concatenate(
        [
            jnp.where(even, other[1:], before),
            jnp.where(even, bucket_order, other[:1]),
            jnp.where(even, other[:1], bucket_order),
        ],
        axis=0,
    )
    message, code = pack(inverse_order, shared_qk, value_rows, out_grad)
    arrived = exchange(message.reshape(PEERS, ROWS, 128))
    returned = exchange(attend(arrived, meta(near, code)))
    return tuple(restore(returned.reshape(CHIPS, 2, ROWS, 128), code))


def solution(mesh):
    rows, orders = P("seq", "head"), P("head", "seq")
    return jax.shard_map(
        per_device,
        mesh=mesh,
        in_specs=(rows, rows, rows, orders, orders),
        out_specs=(rows, rows, rows),
        check_vma=False,
    )
```

```python
import jax
import jax.numpy as jnp
from jax import lax
from jax.experimental import pallas as pl
from jax.experimental.pallas import tpu as pltpu
from jax.sharding import PartitionSpec as P

HEAD_DIM = 64
BLOCK = 512
RANKS = 6
PEERS = 128
CHIPS = 64
ROWS = 24

META_FLOPS = 12 * 10**9

log2_e = 1.4426950408889634
self_score = -100000.0 * log2_e
masked_score = -1000000000.0 * log2_e
norm_eps = 1e-06

F32 = jnp.float32
BF16 = jnp.bfloat16
I32 = jnp.int32


def iota(shape, dim):
    return lax.broadcasted_iota(I32, shape, dim)


def mm(a, b):
    return jnp.dot(a, b, preferred_element_type=F32)


def ones_where(mask):
    return jnp.where(mask, F32(1), F32(0)).astype(BF16)


def column(row):
    return jnp.transpose(jnp.broadcast_to(row.astype(F32), (128, row.shape[1])))


def lanes_equal(index_col, width):
    lane = iota(index_col.shape, 1)
    return jnp.concatenate(
        [ones_where(index_col == lane + 128 * n) for n in range(width // 128)], axis=1
    )


def rows_equal(index_row, height):
    return ones_where(iota((height, index_row.shape[1]), 0) == index_row)


def tiles_of(rows):
    count = rows.shape[0] * 8
    mixed = jnp.concatenate(
        [rows[:, 6:8], rows[:, 14:16], rows[:, 22:24], jnp.zeros_like(rows[:, :2])], axis=1
    )
    tiles = [rows[:, 8 * i : 8 * i + 8] for i in range(3)] + [mixed]
    return [t.reshape(count, 128).astype(BF16) for t in tiles]


def rows_of(tiles, mixed):
    pieces = []
    for i, tile in enumerate(tiles):
        pieces += [tile[:, :6], mixed[:, 2 * i : 2 * i + 2]]
    return jnp.concatenate(pieces, axis=1).astype(BF16)


def pack_kernel(slot_hbm, q_hbm, v_hbm, g_hbm, msg_ref, code_ref, slot_ref, q_ref, v_ref, g_ref, sems):
    copies = [
        pltpu.make_async_copy(src, dst, sems.at[i])
        for i, (src, dst) in enumerate(
            [(slot_hbm, slot_ref), (q_hbm, q_ref), (v_hbm, v_ref), (g_hbm, g_ref)]
        )
    ]
    for copy in copies:
        copy.start()
    copies[0].wait()
    block = slot_ref[...] >> 9
    local = block.shape[1]
    member = iota((PEERS, local), 0) == block
    before = ones_where(iota((local, local), 0) < iota((local, local), 1))
    counts = mm(ones_where(member), before)
    rank = jnp.sum(jnp.where(member, counts, F32(0)), axis=0, keepdims=True)
    code = block * 8 + rank.astype(I32)
    code_ref[...] = code

    def choose(offset):
        shape = (CHIPS, 8, 128)
        want = 16 * iota(shape, 0) + iota(shape, 1) + offset
        want = jnp.where(want < 0, want + 8 * PEERS, want).reshape(CHIPS * 8, 128)
        return jnp.concatenate(
            [ones_where(want == code[:, 128 * n : 128 * n + 128]) for n in range(local // 128)],
            axis=1,
        )

    chosen = [choose(offset) for offset in (-8, 0, 8)]
    for copy in copies[1:]:
        copy.wait()
    q, v, g = q_ref[...], v_ref[...], g_ref[...]
    h0, h1 = slice(0, HEAD_DIM), slice(HEAD_DIM, 2 * HEAD_DIM)
    none = jnp.zeros((local, HEAD_DIM), BF16)
    qv = jnp.concatenate([q[:, h0], v[:, h0], q[:, h1], v[:, h1]], axis=1)
    ga = jnp.concatenate([g[:, h0], none, g[:, h1], none], axis=1)
    gb = jnp.concatenate([none, g[:, h0], none, g[:, h1]], axis=1)
    tiles = [mm(one, qv) for one in chosen]
    mixed = mm(jnp.concatenate(chosen[1:], axis=1), jnp.concatenate([ga, gb], axis=0))
    for c in range(2):
        cols = slice(128 * c, 128 * c + 128)
        msg_ref[:, c] = rows_of(
            [t[:, cols].reshape(CHIPS, 8, 128) for t in tiles],
            mixed[:, cols].reshape(CHIPS, 8, 128),
        )


def meta_kernel(orders_ref, code_ref, table_ref):
    n = BLOCK
    lane = iota((n, n), 1)
    at = iota((1, n), 1)

    def wide(col):
        return jnp.concatenate([col] * (n // 128), axis=1)

    for i in range(3):
        pos = orders_ref[i : i + 1].astype(F32)
        pos_col = wide(column(pos))
        place = jnp.sum(jnp.where(pos_col < pos, F32(1), F32(0)), axis=0, keepdims=True)
        place_col = wide(column(place)).astype(I32)
        ordered = jnp.sum(jnp.where(place_col == lane, pos_col, F32(0)), axis=0, keepdims=True)
        source = ordered.astype(I32) >> 9
        start = (source << 9).astype(F32)
        offset = jnp.sum(
            jnp.where(wide(column(ordered)) < start, F32(1), F32(0)), axis=0, keepdims=True
        )
        table_ref[i : i + 1] = ordered.astype(I32)
        table_ref[i + 3 : i + 4] = source * 8 + at - offset.astype(I32)
    table_ref[6:7] = code_ref[...]
    table_ref[7:8] = jnp.zeros((1, n), I32)


def nt(a, b):
    return lax.dot_general(a, b, (((1,), (1,)), ((), ())), preferred_element_type=F32)


def tn(a, b):
    return lax.dot_general(a, b, (((0,), (0,)), ((), ())), preferred_element_type=F32)


def two_terms(x):
    high = x.astype(BF16)
    return high, (x - high.astype(F32)).astype(BF16)


def attend_kernel(arr_ref, rows_ref, out_ref, give_ref):
    n, half, group = BLOCK, BLOCK // 2, 8 * PEERS
    part_z, part_a, part_b, part_g = tiles_of(arr_ref[...].astype(F32))
    reach = 3 * group // 4

    def take(i, part):
        code = rows_ref[3 + i : 4 + i]
        first, last = slice(0, half), slice(half, n)
        give_ref[i, :reach, first] = rows_equal(code[:, first], reach)
        give_ref[i, group - reach :, last] = rows_equal(code[:, last] - (group - reach), reach)
        return jnp.concatenate(
            [
                tn(part[:reach], give_ref[i, :reach, first]),
                tn(part[group - reach :], give_ref[i, group - reach :, last]),
            ],
            axis=1,
        )

    x_z = take(0, part_z)
    x_a = take(1, jnp.concatenate([part_a, part_g], axis=1))
    x_b = take(2, jnp.concatenate([part_b, part_g], axis=1))
    h = HEAD_DIM
    g_a, g_b = x_a[2 * h : 3 * h], x_b[3 * h :]
    pad = jnp.zeros((14, n), F32)
    ones = jnp.ones((16, n), BF16)

    def block_of(x):
        q, v = x[:h], x[h : 2 * h]
        norm = lax.rsqrt(jnp.sum(q * q, axis=0, keepdims=True) + norm_eps)
        return dict(
            q=q,
            qb=q.astype(BF16),
            vb=jnp.concatenate([v.astype(BF16), ones], axis=0),
            norm=norm,
            scale=norm * log2_e,
            key=(q * norm).astype(BF16),
        )

    block_z, block_a, block_b = [block_of(x) for x in (x_z, x_a, x_b)]

    first, last = slice(0, half), slice(half, n)
    row, col = iota((half, half), 0), iota((half, half), 1)

    def low_high(x):
        return x[:half], x[half:]

    def late(x, y):
        return jnp.concatenate([x[:, first], x[:, last] + y], axis=1)

    def item(prior, own, grads, prior_pos, own_pos):
        q = own["qb"]
        pos = jnp.concatenate([column(own_pos)] * (n // 128), axis=1)
        s0 = tn(q, prior["qb"]) * prior["scale"]
        s0 = jnp.where(prior_pos.astype(F32) < pos, s0, masked_score)
        s1 = tn(q, own["qb"][:, first]) * own["scale"][:, first]
        s2 = tn(q[:, last], own["qb"][:, last]) * own["scale"][:, last]
        yield

        def triangle(s):
            return jnp.where(col < row, s, jnp.where(col == row, self_score, masked_score))

        s1 = jnp.concatenate([triangle(s1[:half]), s1[half:]], axis=0)
        s2 = triangle(s2)
        top0, top1, top2 = (jnp.max(s, axis=1, keepdims=True) for s in (s0, s1, s2))
        top_low, top_high = low_high(jnp.maximum(top0, top1))
        top_high = jnp.maximum(top_high, top2)
        top = jnp.concatenate([top_low, top_high], axis=0)
        p0, p1, p2 = jnp.exp2(s0 - top), jnp.exp2(s1 - top), jnp.exp2(s2 - top_high)
        b0, b1, b2 = p0.astype(BF16), p1.astype(BF16), p2.astype(BF16)
        yield
        v0, v1, v2 = prior["vb"], own["vb"][:, first], own["vb"][:, last]
        summed = late(nt(v0, b0) + nt(v1, b1), nt(v2, b2))
        inverse = 1.0 / summed[h : h + 1]
        out = (summed[:h] * inverse).astype(BF16)
        grad = (grads * inverse).astype(BF16)
        delta = jnp.sum(grad.astype(F32) * out.astype(F32), axis=0, keepdims=True)
        terms = [x.astype(F32) for x in (grad, *two_terms(-delta))]
        left = jnp.concatenate([*terms, pad], axis=0).astype(BF16)
        yield
        d0 = (p0 * tn(left, v0)).astype(BF16)
        d1 = (p1 * tn(left, v1)).astype(BF16)
        d2 = (p2 * tn(left[:, last], v2)).astype(BF16)
        yield
        dq = late(
            nt(prior["key"], d0) + nt(own["key"][:, first], d1), nt(own["key"][:, last], d2)
        )
        sums_prior = (mm(q, d0), mm(grad, b0))
        sums_own = tuple(
            jnp.concatenate([mm(x, lo), mm(x[:, last], hi)], axis=1)
            for x, lo, hi in ((q, d1, d2), (grad, b1, b2))
        )
        yield out, dq, sums_prior, sums_own

    pos_z, pos_a, pos_b = rows_ref[0:1], rows_ref[1:2], rows_ref[2:3]
    items = [
        item(block_z, block_a, g_a, pos_z, pos_a),
        item(block_a, block_b, g_b, pos_a, pos_b),
    ]
    ends = {}
    for i in (0, 0, 1, 0, 1, 0, 1, 0, 1, 1):
        ends[i] = next(items[i])
    out_a, dq_a, sums_z, sums_a = ends[0]
    out_b, dq_b, more_a, sums_b = ends[1]
    sums_a = (sums_a[0] + more_a[0], sums_a[1] + more_a[1])

    def result(block, sums, query_grad):
        dk, dv = sums
        norm, q = block["norm"], block["q"]
        along = jnp.sum(q * dk, axis=0, keepdims=True) * (norm * norm)
        dk = norm * (dk - along * q)
        if query_grad is not None:
            dk = dk + query_grad
        return [dk.astype(BF16), dv.astype(BF16)]

    none = jnp.zeros((h, n), BF16)
    turned = [
        jnp.concatenate(pieces, axis=0)
        for pieces in (
            result(block_z, sums_z, None),
            [*result(block_a, sums_a, dq_a), out_a, none],
            [*result(block_b, sums_b, dq_b), none, out_b],
        )
    ]
    for t, used in enumerate((first, slice(0, n), slice(0, n), last)):
        places = slice(t * group // 4, (t + 1) * group // 4)
        peers = slice(t * PEERS // 4, (t + 1) * PEERS // 4)
        s_z, s_a, s_b = (
            nt(give_ref[i, places, used], x[:, used]).reshape(PEERS // 4, 8, x.shape[0])
            for i, x in enumerate(turned)
        )
        mixed = s_a[:, :, 128:] + s_b[:, :, 128:]
        out_ref[peers] = rows_of([s_z, s_a[:, :, :128], s_b[:, :, :128]], mixed)


def restore_kernel(ret_ref, code_ref, att_ref, dqk_ref, dv_ref):
    code = column(code_ref[...]).astype(I32)
    block, rank = code >> 3, code & 7
    chip, odd = block >> 1, (block & 1) == 1
    group = 8 * CHIPS
    own_at = chip * 8 + rank
    prior_at = jnp.where(odd, ((chip + 1) & (CHIPS - 1)) * 8 + rank, -1)
    chosen = jnp.concatenate(
        [
            lanes_equal(prior_at, group),
            lanes_equal(jnp.where(odd, -1, own_at), group),
            lanes_equal(jnp.where(odd, own_at, -1), group),
        ],
        axis=1,
    )
    tiles = [tiles_of(ret_ref[:, c].astype(F32)) for c in range(2)]
    values = [jnp.concatenate([t[i] for t in tiles], axis=1) for i in range(4)]
    grads = mm(chosen, jnp.concatenate(values[:3], axis=0)).astype(BF16)
    outs = mm(lanes_equal(own_at, group), values[3])
    h = HEAD_DIM
    odd_h = odd[:, :h]
    att_ref[...] = jnp.concatenate(
        [
            jnp.where(odd_h, outs[:, h : 2 * h], outs[:, :h]),
            jnp.where(odd_h, outs[:, 3 * h :], outs[:, 2 * h : 3 * h]),
        ],
        axis=1,
    ).astype(BF16)
    dqk_ref[...] = jnp.concatenate([grads[:, :h], grads[:, 2 * h : 3 * h]], axis=1)
    dv_ref[...] = jnp.concatenate([grads[:, h : 2 * h], grads[:, 3 * h :]], axis=1)


def struct(shape, dtype):
    return jax.ShapeDtypeStruct(shape, dtype)


def params(mib):
    return pltpu.CompilerParams(vmem_limit_bytes=mib * 1024 * 1024)


def in_hbm(x):
    return pltpu.with_memory_space_constraint(x, pltpu.HBM)


def pack(slots, q, v, g):
    n = q.shape[0]
    return pl.pallas_call(
        pack_kernel,
        in_specs=[pl.BlockSpec(memory_space=pltpu.HBM)] * 4,
        out_shape=(struct((CHIPS, 2, ROWS, 128), BF16), struct((1, n), I32)),
        scratch_shapes=[pltpu.VMEM((1, n), I32)]
        + [pltpu.VMEM((n, 128), BF16)] * 3
        + [pltpu.SemaphoreType.DMA((4,))],
        compiler_params=params(24),
        name="pack",
    )(*map(in_hbm, (slots, q, v, g)))


def meta(orders, code):
    return pl.pallas_call(
        meta_kernel,
        out_shape=struct((8, BLOCK), I32),
        compiler_params=params(24),
        cost_estimate=pl.CostEstimate(
            flops=META_FLOPS, bytes_accessed=32768, transcendentals=0
        ),
        name="meta",
    )(orders, code)


def attend(arrived, table):
    shape = (PEERS, ROWS, 128)
    return pl.pallas_call(
        attend_kernel,
        out_shape=struct(shape, BF16),
        scratch_shapes=[
            pltpu.VMEM((3, 8 * PEERS, BLOCK), BF16),
        ],
        compiler_params=params(40),
        name="attend",
    )(arrived, table)


def restore(returned, code):
    n = code.shape[1]
    return pl.pallas_call(
        restore_kernel,
        out_shape=[struct((n, 128), BF16)] * 3,
        compiler_params=params(24),
        name="restore",
    )(returned, code)


def exchange(message):
    return lax.all_to_all(message, "seq", split_axis=0, concat_axis=0, tiled=True)


def per_device(shared_qk, value_rows, out_grad, bucket_order, inverse_order):
    peers = range(PEERS)
    before = lax.ppermute(bucket_order, "seq", [(i, (i + 2) % PEERS) for i in peers])
    held = jnp.concatenate([bucket_order, before], axis=0)
    other = lax.ppermute(held, "seq", [(i, i ^ 1) for i in peers])
    even = lax.axis_index("seq") & 1 == 0
    near = jnp.concatenate(
        [
            jnp.where(even, other[1:], before),
            jnp.where(even, bucket_order, other[:1]),
            jnp.where(even, other[:1], bucket_order),
        ],
        axis=0,
    )
    message, code = pack(inverse_order, shared_qk, value_rows, out_grad)
    arrived = exchange(message.reshape(PEERS, ROWS, 128))
    returned = exchange(attend(arrived, meta(near, code)))
    return tuple(restore(returned.reshape(CHIPS, 2, ROWS, 128), code))


def solution(mesh):
    rows, orders = P("seq", "head"), P("head", "seq")
    return jax.shard_map(
        per_device,
        mesh=mesh,
        in_specs=(rows, rows, rows, orders, orders),
        out_specs=(rows, rows, rows),
        check_vma=False,
    )
```

```python
import jax
import jax.numpy as jnp
from jax import lax
from jax.experimental import pallas as pl
from jax.experimental.pallas import tpu as pltpu
from jax.sharding import PartitionSpec as P

HEAD_DIM = 64
BLOCK = 512
RANKS = 6
PEERS = 128
CHIPS = 64
ROWS = 24

META_FLOPS = 12 * 10**9

log2_e = 1.4426950408889634
self_score = -100000.0 * log2_e
masked_score = -1000000000.0 * log2_e
norm_eps = 1e-06

F32 = jnp.float32
BF16 = jnp.bfloat16
I32 = jnp.int32


def iota(shape, dim):
    return lax.broadcasted_iota(I32, shape, dim)


def mm(a, b):
    return jnp.dot(a, b, preferred_element_type=F32)


def ones_where(mask):
    return jnp.where(mask, F32(1), F32(0)).astype(BF16)


def column(row):
    return jnp.transpose(jnp.broadcast_to(row.astype(F32), (128, row.shape[1])))


def lanes_equal(index_col, width):
    lane = iota(index_col.shape, 1)
    return jnp.concatenate(
        [ones_where(index_col == lane + 128 * n) for n in range(width // 128)], axis=1
    )


def rows_equal(index_row, height):
    return ones_where(iota((height, index_row.shape[1]), 0) == index_row)


def tiles_of(rows):
    count = rows.shape[0] * 8
    mixed = jnp.concatenate(
        [rows[:, 6:8], rows[:, 14:16], rows[:, 22:24], jnp.zeros_like(rows[:, :2])], axis=1
    )
    tiles = [rows[:, 8 * i : 8 * i + 8] for i in range(3)] + [mixed]
    return [t.reshape(count, 128).astype(BF16) for t in tiles]


def rows_of(tiles, mixed):
    pieces = []
    for i, tile in enumerate(tiles):
        pieces += [tile[:, :6], mixed[:, 2 * i : 2 * i + 2]]
    return jnp.concatenate(pieces, axis=1).astype(BF16)


def pack_kernel(slot_hbm, q_hbm, v_hbm, g_hbm, msg_ref, code_ref, slot_ref, q_ref, v_ref, g_ref, sems):
    copies = [
        pltpu.make_async_copy(src, dst, sems.at[i])
        for i, (src, dst) in enumerate(
            [(slot_hbm, slot_ref), (q_hbm, q_ref), (v_hbm, v_ref), (g_hbm, g_ref)]
        )
    ]
    for copy in copies:
        copy.start()
    copies[0].wait()
    block = slot_ref[...] >> 9
    local = block.shape[1]
    member = iota((PEERS, local), 0) == block
    before = ones_where(iota((local, local), 0) < iota((local, local), 1))
    counts = mm(ones_where(member), before)
    rank = jnp.sum(jnp.where(member, counts, F32(0)), axis=0, keepdims=True)
    code = block * 8 + rank.astype(I32)
    code_ref[...] = code

    def choose(offset):
        shape = (CHIPS, 8, 128)
        want = 16 * iota(shape, 0) + iota(shape, 1) + offset
        want = jnp.where(want < 0, want + 8 * PEERS, want).reshape(CHIPS * 8, 128)
        return jnp.concatenate(
            [ones_where(want == code[:, 128 * n : 128 * n + 128]) for n in range(local // 128)],
            axis=1,
        )

    chosen = [choose(offset) for offset in (-8, 0, 8)]
    for copy in copies[1:]:
        copy.wait()
    q, v, g = q_ref[...], v_ref[...], g_ref[...]
    h0, h1 = slice(0, HEAD_DIM), slice(HEAD_DIM, 2 * HEAD_DIM)
    none = jnp.zeros((local, HEAD_DIM), BF16)
    qv = jnp.concatenate([q[:, h0], v[:, h0], q[:, h1], v[:, h1]], axis=1)
    ga = jnp.concatenate([g[:, h0], none, g[:, h1], none], axis=1)
    gb = jnp.concatenate([none, g[:, h0], none, g[:, h1]], axis=1)
    tiles = [mm(one, qv) for one in chosen]
    mixed = mm(jnp.concatenate(chosen[1:], axis=1), jnp.concatenate([ga, gb], axis=0))
    for c in range(2):
        cols = slice(128 * c, 128 * c + 128)
        msg_ref[:, c] = rows_of(
            [t[:, cols].reshape(CHIPS, 8, 128) for t in tiles],
            mixed[:, cols].reshape(CHIPS, 8, 128),
        )


def meta_kernel(orders_ref, code_ref, table_ref):
    n = BLOCK
    lane = iota((n, n), 1)
    at = iota((1, n), 1)

    def wide(col):
        return jnp.concatenate([col] * (n // 128), axis=1)

    for i in range(3):
        pos = orders_ref[i : i + 1].astype(F32)
        pos_col = wide(column(pos))
        place = jnp.sum(jnp.where(pos_col < pos, F32(1), F32(0)), axis=0, keepdims=True)
        place_col = wide(column(place)).astype(I32)
        ordered = jnp.sum(jnp.where(place_col == lane, pos_col, F32(0)), axis=0, keepdims=True)
        source = ordered.astype(I32) >> 9
        start = (source << 9).astype(F32)
        offset = jnp.sum(
            jnp.where(wide(column(ordered)) < start, F32(1), F32(0)), axis=0, keepdims=True
        )
        table_ref[i : i + 1] = ordered.astype(I32)
        table_ref[i + 3 : i + 4] = source * 8 + at - offset.astype(I32)
    table_ref[6:7] = code_ref[...]
    table_ref[7:8] = jnp.zeros((1, n), I32)


def nt(a, b):
    return lax.dot_general(a, b, (((1,), (1,)), ((), ())), preferred_element_type=F32)


def tn(a, b):
    return lax.dot_general(a, b, (((0,), (0,)), ((), ())), preferred_element_type=F32)


def two_terms(x):
    high = x.astype(BF16)
    return high, (x - high.astype(F32)).astype(BF16)


def attend_kernel(arr_ref, rows_ref, out_ref, give_ref):
    n, half, group = BLOCK, BLOCK // 2, 8 * PEERS
    part_z, part_a, part_b, part_g = tiles_of(arr_ref[...].astype(F32))
    reach = 3 * group // 4

    def take(i, part):
        code = rows_ref[3 + i : 4 + i]
        first, last = slice(0, half), slice(half, n)
        give_ref[i, :reach, first] = rows_equal(code[:, first], reach)
        give_ref[i, group - reach :, last] = rows_equal(code[:, last] - (group - reach), reach)
        return jnp.concatenate(
            [
                tn(part[:reach], give_ref[i, :reach, first]),
                tn(part[group - reach :], give_ref[i, group - reach :, last]),
            ],
            axis=1,
        )

    x_z = take(0, part_z)
    x_a = take(1, jnp.concatenate([part_a, part_g], axis=1))
    x_b = take(2, jnp.concatenate([part_b, part_g], axis=1))
    h = HEAD_DIM
    g_a, g_b = x_a[2 * h : 3 * h], x_b[3 * h :]
    pad = jnp.zeros((14, n), F32)
    ones = jnp.ones((16, n), BF16)

    def block_of(x):
        q, v = x[:h], x[h : 2 * h]
        norm = lax.rsqrt(jnp.sum(q * q, axis=0, keepdims=True) + norm_eps)
        return dict(
            q=q,
            qb=q.astype(BF16),
            vb=jnp.concatenate([v.astype(BF16), ones], axis=0),
            norm=norm,
            scale=norm * log2_e,
            key=(q * norm).astype(BF16),
        )

    block_z, block_a, block_b = [block_of(x) for x in (x_z, x_a, x_b)]

    first, last = slice(0, half), slice(half, n)
    row, col = iota((half, half), 0), iota((half, half), 1)

    def low_high(x):
        return x[:half], x[half:]

    def late(x, y):
        return jnp.concatenate([x[:, first], x[:, last] + y], axis=1)

    def item(prior, own, grads, prior_pos, own_pos):
        q = own["qb"]
        pos = jnp.concatenate([column(own_pos)] * (n // 128), axis=1)

        def most(name):
            return jnp.concatenate([prior[name], own[name][:, first]], axis=1)

        v1, v2 = most("vb"), own["vb"][:, last]
        s1 = tn(q, most("qb")) * most("scale")
        s2 = tn(q[:, last], own["qb"][:, last]) * own["scale"][:, last]
        yield

        def triangle(s):
            return jnp.where(col < row, s, jnp.where(col == row, self_score, masked_score))

        s0 = jnp.where(prior_pos.astype(F32) < pos, s1[:, :n], masked_score)
        s1 = jnp.concatenate([triangle(s1[:half, n:]), s1[half:, n:]], axis=0)
        s2 = triangle(s2)
        top0, top1, top2 = (jnp.max(s, axis=1, keepdims=True) for s in (s0, s1, s2))
        top_low, top_high = low_high(jnp.maximum(top0, top1))
        top_high = jnp.maximum(top_high, top2)
        top = jnp.concatenate([top_low, top_high], axis=0)
        p1 = jnp.concatenate([jnp.exp2(s0 - top), jnp.exp2(s1 - top)], axis=1)
        p2 = jnp.exp2(s2 - top_high)
        b1, b2 = p1.astype(BF16), p2.astype(BF16)
        yield
        summed = late(nt(v1, b1), nt(v2, b2))
        inverse = 1.0 / summed[h : h + 1]
        out = (summed[:h] * inverse).astype(BF16)
        grad = (grads * inverse).astype(BF16)
        delta = jnp.sum(grad.astype(F32) * out.astype(F32), axis=0, keepdims=True)
        terms = [x.astype(F32) for x in (grad, *two_terms(-delta))]
        left = jnp.concatenate([*terms, pad], axis=0).astype(BF16)
        yield
        d1 = (p1 * tn(left, v1)).astype(BF16)
        d2 = (p2 * tn(left[:, last], v2)).astype(BF16)
        yield
        dq = late(nt(most("key"), d1), nt(own["key"][:, last], d2))
        sums = [(mm(x, lo), mm(x[:, last], hi)) for x, lo, hi in ((q, d1, d2), (grad, b1, b2))]
        sums_prior = tuple(lo[:, :n] for lo, _ in sums)
        sums_own = tuple(jnp.concatenate([lo[:, n:], hi], axis=1) for lo, hi in sums)
        yield out, dq, sums_prior, sums_own

    pos_z, pos_a, pos_b = rows_ref[0:1], rows_ref[1:2], rows_ref[2:3]
    items = [
        item(block_z, block_a, g_a, pos_z, pos_a),
        item(block_a, block_b, g_b, pos_a, pos_b),
    ]
    ends = {}
    for i in (0, 0, 1, 0, 1, 0, 1, 0, 1, 1):
        ends[i] = next(items[i])
    out_a, dq_a, sums_z, sums_a = ends[0]
    out_b, dq_b, more_a, sums_b = ends[1]
    sums_a = (sums_a[0] + more_a[0], sums_a[1] + more_a[1])

    def result(block, sums, query_grad):
        dk, dv = sums
        norm, q = block["norm"], block["q"]
        along = jnp.sum(q * dk, axis=0, keepdims=True) * (norm * norm)
        dk = norm * (dk - along * q)
        if query_grad is not None:
            dk = dk + query_grad
        return [dk.astype(BF16), dv.astype(BF16)]

    none = jnp.zeros((h, n), BF16)
    turned = [
        jnp.concatenate(pieces, axis=0)
        for pieces in (
            result(block_z, sums_z, None),
            [*result(block_a, sums_a, dq_a), out_a, none],
            [*result(block_b, sums_b, dq_b), none, out_b],
        )
    ]
    for t, used in enumerate((first, slice(0, n), slice(0, n), last)):
        places = slice(t * group // 4, (t + 1) * group // 4)
        peers = slice(t * PEERS // 4, (t + 1) * PEERS // 4)
        s_z, s_a, s_b = (
            nt(give_ref[i, places, used], x[:, used]).reshape(PEERS // 4, 8, x.shape[0])
            for i, x in enumerate(turned)
        )
        mixed = s_a[:, :, 128:] + s_b[:, :, 128:]
        out_ref[peers] = rows_of([s_z, s_a[:, :, :128], s_b[:, :, :128]], mixed)


def restore_kernel(ret_ref, code_ref, att_ref, dqk_ref, dv_ref):
    code = column(code_ref[...]).astype(I32)
    block, rank = code >> 3, code & 7
    chip, odd = block >> 1, (block & 1) == 1
    group = 8 * CHIPS
    own_at = chip * 8 + rank
    prior_at = jnp.where(odd, ((chip + 1) & (CHIPS - 1)) * 8 + rank, -1)
    chosen = jnp.concatenate(
        [
            lanes_equal(prior_at, group),
            lanes_equal(jnp.where(odd, -1, own_at), group),
            lanes_equal(jnp.where(odd, own_at, -1), group),
        ],
        axis=1,
    )
    tiles = [tiles_of(ret_ref[:, c].astype(F32)) for c in range(2)]
    values = [jnp.concatenate([t[i] for t in tiles], axis=1) for i in range(4)]
    grads = mm(chosen, jnp.concatenate(values[:3], axis=0)).astype(BF16)
    outs = mm(lanes_equal(own_at, group), values[3])
    h = HEAD_DIM
    odd_h = odd[:, :h]
    att_ref[...] = jnp.concatenate(
        [
            jnp.where(odd_h, outs[:, h : 2 * h], outs[:, :h]),
            jnp.where(odd_h, outs[:, 3 * h :], outs[:, 2 * h : 3 * h]),
        ],
        axis=1,
    ).astype(BF16)
    dqk_ref[...] = jnp.concatenate([grads[:, :h], grads[:, 2 * h : 3 * h]], axis=1)
    dv_ref[...] = jnp.concatenate([grads[:, h : 2 * h], grads[:, 3 * h :]], axis=1)


def struct(shape, dtype):
    return jax.ShapeDtypeStruct(shape, dtype)


def params(mib):
    return pltpu.CompilerParams(vmem_limit_bytes=mib * 1024 * 1024)


def in_hbm(x):
    return pltpu.with_memory_space_constraint(x, pltpu.HBM)


def pack(slots, q, v, g):
    n = q.shape[0]
    return pl.pallas_call(
        pack_kernel,
        in_specs=[pl.BlockSpec(memory_space=pltpu.HBM)] * 4,
        out_shape=(struct((CHIPS, 2, ROWS, 128), BF16), struct((1, n), I32)),
        scratch_shapes=[pltpu.VMEM((1, n), I32)]
        + [pltpu.VMEM((n, 128), BF16)] * 3
        + [pltpu.SemaphoreType.DMA((4,))],
        compiler_params=params(24),
        name="pack",
    )(*map(in_hbm, (slots, q, v, g)))


def meta(orders, code):
    return pl.pallas_call(
        meta_kernel,
        out_shape=struct((8, BLOCK), I32),
        compiler_params=params(24),
        cost_estimate=pl.CostEstimate(
            flops=META_FLOPS, bytes_accessed=32768, transcendentals=0
        ),
        name="meta",
    )(orders, code)


def attend(arrived, table):
    shape = (PEERS, ROWS, 128)
    return pl.pallas_call(
        attend_kernel,
        out_shape=struct(shape, BF16),
        scratch_shapes=[
            pltpu.VMEM((3, 8 * PEERS, BLOCK), BF16),
        ],
        compiler_params=params(40),
        name="attend",
    )(arrived, table)


def restore(returned, code):
    n = code.shape[1]
    return pl.pallas_call(
        restore_kernel,
        out_shape=[struct((n, 128), BF16)] * 3,
        compiler_params=params(24),
        name="restore",
    )(returned, code)


def exchange(message):
    return lax.all_to_all(message, "seq", split_axis=0, concat_axis=0, tiled=True)


def per_device(shared_qk, value_rows, out_grad, bucket_order, inverse_order):
    peers = range(PEERS)
    before = lax.ppermute(bucket_order, "seq", [(i, (i + 2) % PEERS) for i in peers])
    held = jnp.concatenate([bucket_order, before], axis=0)
    other = lax.ppermute(held, "seq", [(i, i ^ 1) for i in peers])
    even = lax.axis_index("seq") & 1 == 0
    near = jnp.concatenate(
        [
            jnp.where(even, other[1:], before),
            jnp.where(even, bucket_order, other[:1]),
            jnp.where(even, other[:1], bucket_order),
        ],
        axis=0,
    )
    message, code = pack(inverse_order, shared_qk, value_rows, out_grad)
    arrived = exchange(message.reshape(PEERS, ROWS, 128))
    returned = exchange(attend(arrived, meta(near, code)))
    return tuple(restore(returned.reshape(CHIPS, 2, ROWS, 128), code))


def solution(mesh):
    rows, orders = P("seq", "head"), P("head", "seq")
    return jax.shard_map(
        per_device,
        mesh=mesh,
        in_specs=(rows, rows, rows, orders, orders),
        out_specs=(rows, rows, rows),
        check_vma=False,
    )
```

```python
import jax
import jax.numpy as jnp
from jax import lax
from jax.experimental import pallas as pl
from jax.experimental.pallas import tpu as pltpu
from jax.sharding import PartitionSpec as P

HEAD_DIM = 64
BLOCK = 512
RANKS = 6
PEERS = 128
CHIPS = 64
ROWS = 24

META_FLOPS = 12 * 10**9

log2_e = 1.4426950408889634
self_score = -100000.0 * log2_e
masked_score = -1000000000.0 * log2_e
norm_eps = 1e-06

F32 = jnp.float32
BF16 = jnp.bfloat16
I32 = jnp.int32


def iota(shape, dim):
    return lax.broadcasted_iota(I32, shape, dim)


def mm(a, b):
    return jnp.dot(a, b, preferred_element_type=F32)


def ones_where(mask):
    return jnp.where(mask, F32(1), F32(0)).astype(BF16)


def column(row):
    return jnp.transpose(jnp.broadcast_to(row.astype(F32), (128, row.shape[1])))


def lanes_equal(index_col, width):
    lane = iota(index_col.shape, 1)
    return jnp.concatenate(
        [ones_where(index_col == lane + 128 * n) for n in range(width // 128)], axis=1
    )


def rows_equal(index_row, height):
    return ones_where(iota((height, index_row.shape[1]), 0) == index_row)


def tiles_of(rows):
    count = rows.shape[0] * 8
    mixed = jnp.concatenate(
        [rows[:, 6:8], rows[:, 14:16], rows[:, 22:24], jnp.zeros_like(rows[:, :2])], axis=1
    )
    tiles = [rows[:, 8 * i : 8 * i + 8] for i in range(3)] + [mixed]
    return [t.reshape(count, 128).astype(BF16) for t in tiles]


def rows_of(tiles, mixed):
    pieces = []
    for i, tile in enumerate(tiles):
        pieces += [tile[:, :6], mixed[:, 2 * i : 2 * i + 2]]
    return jnp.concatenate(pieces, axis=1).astype(BF16)


def pack_kernel(slot_hbm, q_hbm, v_hbm, g_hbm, msg_ref, code_ref, slot_ref, q_ref, v_ref, g_ref, sems):
    copies = [
        pltpu.make_async_copy(src, dst, sems.at[i])
        for i, (src, dst) in enumerate(
            [(slot_hbm, slot_ref), (q_hbm, q_ref), (v_hbm, v_ref), (g_hbm, g_ref)]
        )
    ]
    for i, copy in enumerate(copies):
        copy.start(priority=int(i == 0))
    copies[0].wait()
    block = slot_ref[...] >> 9
    local = block.shape[1]
    member = iota((PEERS, local), 0) == block
    before = ones_where(iota((local, local), 0) < iota((local, local), 1))
    counts = mm(ones_where(member), before)
    rank = jnp.sum(jnp.where(member, counts, F32(0)), axis=0, keepdims=True)
    code = block * 8 + rank.astype(I32)
    code_ref[...] = code

    def choose(offset):
        shape = (CHIPS, 8, 128)
        want = 16 * iota(shape, 0) + iota(shape, 1) + offset
        want = jnp.where(want < 0, want + 8 * PEERS, want).reshape(CHIPS * 8, 128)
        return jnp.concatenate(
            [ones_where(want == code[:, 128 * n : 128 * n + 128]) for n in range(local // 128)],
            axis=1,
        )

    chosen = [choose(offset) for offset in (-8, 0, 8)]
    for copy in copies[1:]:
        copy.wait()
    q, v, g = q_ref[...], v_ref[...], g_ref[...]
    h0, h1 = slice(0, HEAD_DIM), slice(HEAD_DIM, 2 * HEAD_DIM)
    none = jnp.zeros((local, HEAD_DIM), BF16)
    qv = jnp.concatenate([q[:, h0], v[:, h0], q[:, h1], v[:, h1]], axis=1)
    ga = jnp.concatenate([g[:, h0], none, g[:, h1], none], axis=1)
    gb = jnp.concatenate([none, g[:, h0], none, g[:, h1]], axis=1)
    tiles = [mm(one, qv) for one in chosen]
    mixed = mm(jnp.concatenate(chosen[1:], axis=1), jnp.concatenate([ga, gb], axis=0))
    for c in range(2):
        cols = slice(128 * c, 128 * c + 128)
        msg_ref[:, c] = rows_of(
            [t[:, cols].reshape(CHIPS, 8, 128) for t in tiles],
            mixed[:, cols].reshape(CHIPS, 8, 128),
        )


def meta_kernel(orders_ref, code_ref, table_ref):
    n = BLOCK
    lane = iota((n, n), 1)
    at = iota((1, n), 1)

    def wide(col):
        return jnp.concatenate([col] * (n // 128), axis=1)

    for i in range(3):
        pos = orders_ref[i : i + 1].astype(F32)
        pos_col = wide(column(pos))
        place = jnp.sum(jnp.where(pos_col < pos, F32(1), F32(0)), axis=0, keepdims=True)
        place_col = wide(column(place)).astype(I32)
        ordered = jnp.sum(jnp.where(place_col == lane, pos_col, F32(0)), axis=0, keepdims=True)
        source = ordered.astype(I32) >> 9
        start = (source << 9).astype(F32)
        offset = jnp.sum(
            jnp.where(wide(column(ordered)) < start, F32(1), F32(0)), axis=0, keepdims=True
        )
        table_ref[i : i + 1] = ordered.astype(I32)
        table_ref[i + 3 : i + 4] = source * 8 + at - offset.astype(I32)
    table_ref[6:7] = code_ref[...]
    table_ref[7:8] = jnp.zeros((1, n), I32)


def nt(a, b):
    return lax.dot_general(a, b, (((1,), (1,)), ((), ())), preferred_element_type=F32)


def tn(a, b):
    return lax.dot_general(a, b, (((0,), (0,)), ((), ())), preferred_element_type=F32)


def two_terms(x):
    high = x.astype(BF16)
    return high, (x - high.astype(F32)).astype(BF16)


def attend_kernel(arr_ref, rows_ref, out_ref, give_ref):
    n, half, group = BLOCK, BLOCK // 2, 8 * PEERS
    part_z, part_a, part_b, part_g = tiles_of(arr_ref[...].astype(F32))
    reach = 3 * group // 4

    def take(i, part):
        code = rows_ref[3 + i : 4 + i]
        first, last = slice(0, half), slice(half, n)
        give_ref[i, :reach, first] = rows_equal(code[:, first], reach)
        give_ref[i, group - reach :, last] = rows_equal(code[:, last] - (group - reach), reach)
        return jnp.concatenate(
            [
                tn(part[:reach], give_ref[i, :reach, first]),
                tn(part[group - reach :], give_ref[i, group - reach :, last]),
            ],
            axis=1,
        )

    x_z = take(0, part_z)
    x_a = take(1, jnp.concatenate([part_a, part_g], axis=1))
    x_b = take(2, jnp.concatenate([part_b, part_g], axis=1))
    h = HEAD_DIM
    g_a, g_b = x_a[2 * h : 3 * h], x_b[3 * h :]
    pad = jnp.zeros((14, n), F32)
    ones = jnp.ones((16, n), BF16)

    def block_of(x):
        q, v = x[:h], x[h : 2 * h]
        norm = lax.rsqrt(jnp.sum(q * q, axis=0, keepdims=True) + norm_eps)
        return dict(
            q=q,
            qb=q.astype(BF16),
            vb=jnp.concatenate([v.astype(BF16), ones], axis=0),
            norm=norm,
            scale=norm * log2_e,
            key=(q * norm).astype(BF16),
        )

    block_z, block_a, block_b = [block_of(x) for x in (x_z, x_a, x_b)]

    first, last = slice(0, half), slice(half, n)
    row, col = iota((half, half), 0), iota((half, half), 1)

    def low_high(x):
        return x[:half], x[half:]

    def late(x, y):
        return jnp.concatenate([x[:, first], x[:, last] + y], axis=1)

    def item(prior, own, grads, prior_pos, own_pos):
        q = own["qb"]
        pos = jnp.concatenate([column(own_pos)] * (n // 128), axis=1)
        s0 = tn(q, prior["qb"]) * prior["scale"]
        s0 = jnp.where(prior_pos.astype(F32) < pos, s0, masked_score)
        s1 = tn(q, own["qb"][:, first]) * own["scale"][:, first]
        s2 = tn(q[:, last], own["qb"][:, last]) * own["scale"][:, last]
        yield

        def triangle(s):
            return jnp.where(col < row, s, jnp.where(col == row, self_score, masked_score))

        s1 = jnp.concatenate([triangle(s1[:half]), s1[half:]], axis=0)
        s2 = triangle(s2)
        top0, top1, top2 = (jnp.max(s, axis=1, keepdims=True) for s in (s0, s1, s2))
        top_low, top_high = low_high(jnp.maximum(top0, top1))
        top_high = jnp.maximum(top_high, top2)
        top = jnp.concatenate([top_low, top_high], axis=0)
        p0, p1, p2 = jnp.exp2(s0 - top), jnp.exp2(s1 - top), jnp.exp2(s2 - top_high)
        b0, b1, b2 = p0.astype(BF16), p1.astype(BF16), p2.astype(BF16)
        yield
        v0, v1, v2 = prior["vb"], own["vb"][:, first], own["vb"][:, last]
        summed = late(nt(v0, b0) + nt(v1, b1), nt(v2, b2))
        inverse = 1.0 / summed[h : h + 1]
        out = (summed[:h] * inverse).astype(BF16)
        grad = (grads * inverse).astype(BF16)
        delta = jnp.sum(grad.astype(F32) * out.astype(F32), axis=0, keepdims=True)
        terms = [x.astype(F32) for x in (grad, *two_terms(-delta))]
        left = jnp.concatenate([*terms, pad], axis=0).astype(BF16)
        yield
        d0 = (p0 * tn(left, v0)).astype(BF16)
        d1 = (p1 * tn(left, v1)).astype(BF16)
        d2 = (p2 * tn(left[:, last], v2)).astype(BF16)
        yield
        dq = late(
            nt(prior["key"], d0) + nt(own["key"][:, first], d1), nt(own["key"][:, last], d2)
        )
        sums_prior = (mm(q, d0), mm(grad, b0))
        sums_own = tuple(
            jnp.concatenate([mm(x, lo), mm(x[:, last], hi)], axis=1)
            for x, lo, hi in ((q, d1, d2), (grad, b1, b2))
        )
        yield out, dq, sums_prior, sums_own

    pos_z, pos_a, pos_b = rows_ref[0:1], rows_ref[1:2], rows_ref[2:3]
    items = [
        item(block_z, block_a, g_a, pos_z, pos_a),
        item(block_a, block_b, g_b, pos_a, pos_b),
    ]
    ends = {}
    for i in (0, 0, 1, 0, 1, 0, 1, 0, 1, 1):
        ends[i] = next(items[i])
    out_a, dq_a, sums_z, sums_a = ends[0]
    out_b, dq_b, more_a, sums_b = ends[1]
    sums_a = (sums_a[0] + more_a[0], sums_a[1] + more_a[1])

    def result(block, sums, query_grad):
        dk, dv = sums
        norm, q = block["norm"], block["q"]
        along = jnp.sum(q * dk, axis=0, keepdims=True) * (norm * norm)
        dk = norm * (dk - along * q)
        if query_grad is not None:
            dk = dk + query_grad
        return [dk.astype(BF16), dv.astype(BF16)]

    none = jnp.zeros((h, n), BF16)
    turned = [
        jnp.concatenate(pieces, axis=0)
        for pieces in (
            result(block_z, sums_z, None),
            [*result(block_a, sums_a, dq_a), out_a, none],
            [*result(block_b, sums_b, dq_b), none, out_b],
        )
    ]
    for t, used in enumerate((first, slice(0, n), slice(0, n), last)):
        places = slice(t * group // 4, (t + 1) * group // 4)
        peers = slice(t * PEERS // 4, (t + 1) * PEERS // 4)
        s_z, s_a, s_b = (
            nt(give_ref[i, places, used], x[:, used]).reshape(PEERS // 4, 8, x.shape[0])
            for i, x in enumerate(turned)
        )
        mixed = s_a[:, :, 128:] + s_b[:, :, 128:]
        out_ref[peers] = rows_of([s_z, s_a[:, :, :128], s_b[:, :, :128]], mixed)


def restore_kernel(ret_ref, code_ref, att_ref, dqk_ref, dv_ref):
    code = column(code_ref[...]).astype(I32)
    block, rank = code >> 3, code & 7
    chip, odd = block >> 1, (block & 1) == 1
    group = 8 * CHIPS
    own_at = chip * 8 + rank
    prior_at = jnp.where(odd, ((chip + 1) & (CHIPS - 1)) * 8 + rank, -1)
    chosen = jnp.concatenate(
        [
            lanes_equal(prior_at, group),
            lanes_equal(jnp.where(odd, -1, own_at), group),
            lanes_equal(jnp.where(odd, own_at, -1), group),
        ],
        axis=1,
    )
    tiles = [tiles_of(ret_ref[:, c].astype(F32)) for c in range(2)]
    values = [jnp.concatenate([t[i] for t in tiles], axis=1) for i in range(4)]
    grads = mm(chosen, jnp.concatenate(values[:3], axis=0)).astype(BF16)
    outs = mm(lanes_equal(own_at, group), values[3])
    h = HEAD_DIM
    odd_h = odd[:, :h]
    att_ref[...] = jnp.concatenate(
        [
            jnp.where(odd_h, outs[:, h : 2 * h], outs[:, :h]),
            jnp.where(odd_h, outs[:, 3 * h :], outs[:, 2 * h : 3 * h]),
        ],
        axis=1,
    ).astype(BF16)
    dqk_ref[...] = jnp.concatenate([grads[:, :h], grads[:, 2 * h : 3 * h]], axis=1)
    dv_ref[...] = jnp.concatenate([grads[:, h : 2 * h], grads[:, 3 * h :]], axis=1)


def struct(shape, dtype):
    return jax.ShapeDtypeStruct(shape, dtype)


def params(mib):
    return pltpu.CompilerParams(vmem_limit_bytes=mib * 1024 * 1024)


def in_hbm(x):
    return pltpu.with_memory_space_constraint(x, pltpu.HBM)


def pack(slots, q, v, g):
    n = q.shape[0]
    return pl.pallas_call(
        pack_kernel,
        in_specs=[pl.BlockSpec(memory_space=pltpu.HBM)] * 4,
        out_shape=(struct((CHIPS, 2, ROWS, 128), BF16), struct((1, n), I32)),
        scratch_shapes=[pltpu.VMEM((1, n), I32)]
        + [pltpu.VMEM((n, 128), BF16)] * 3
        + [pltpu.SemaphoreType.DMA((4,))],
        compiler_params=params(24),
        name="pack",
    )(*map(in_hbm, (slots, q, v, g)))


def meta(orders, code):
    return pl.pallas_call(
        meta_kernel,
        out_shape=struct((8, BLOCK), I32),
        compiler_params=params(24),
        cost_estimate=pl.CostEstimate(
            flops=META_FLOPS, bytes_accessed=32768, transcendentals=0
        ),
        name="meta",
    )(orders, code)


def attend(arrived, table):
    shape = (PEERS, ROWS, 128)
    return pl.pallas_call(
        attend_kernel,
        out_shape=struct(shape, BF16),
        scratch_shapes=[
            pltpu.VMEM((3, 8 * PEERS, BLOCK), BF16),
        ],
        compiler_params=params(40),
        name="attend",
    )(arrived, table)


def restore(returned, code):
    n = code.shape[1]
    return pl.pallas_call(
        restore_kernel,
        out_shape=[struct((n, 128), BF16)] * 3,
        compiler_params=params(24),
        name="restore",
    )(returned, code)


def exchange(message):
    return lax.all_to_all(message, "seq", split_axis=0, concat_axis=0, tiled=True)


def per_device(shared_qk, value_rows, out_grad, bucket_order, inverse_order):
    peers = range(PEERS)
    before = lax.ppermute(bucket_order, "seq", [(i, (i + 2) % PEERS) for i in peers])
    held = jnp.concatenate([bucket_order, before], axis=0)
    other = lax.ppermute(held, "seq", [(i, i ^ 1) for i in peers])
    even = lax.axis_index("seq") & 1 == 0
    near = jnp.concatenate(
        [
            jnp.where(even, other[1:], before),
            jnp.where(even, bucket_order, other[:1]),
            jnp.where(even, other[:1], bucket_order),
        ],
        axis=0,
    )
    message, code = pack(inverse_order, shared_qk, value_rows, out_grad)
    arrived = exchange(message.reshape(PEERS, ROWS, 128))
    returned = exchange(attend(arrived, meta(near, code)))
    return tuple(restore(returned.reshape(CHIPS, 2, ROWS, 128), code))


def solution(mesh):
    rows, orders = P("seq", "head"), P("head", "seq")
    return jax.shard_map(
        per_device,
        mesh=mesh,
        in_specs=(rows, rows, rows, orders, orders),
        out_specs=(rows, rows, rows),
        check_vma=False,
    )
```
